32 devices in a mesh: seq: 8 (over z, y), tp: 4 (over x, core).
Axes of the slice: x: 2, y: 2, z: 4, core: 2. Of those that a mesh axis runs over, the one named last changes fastest.
Arguments:
- q_new: bfloat16 [4096, 8192], P('seq', 'tp'), may hold values from -16 to 16
- k_new: bfloat16 [4096, 1024], P('seq', 'tp'), may hold values from -6 to 6
- v_new: bfloat16 [4096, 1024], P('seq', 'tp'), may hold values from -6 to 6
- q_bias: bfloat16 [8192], P('tp'), may hold values from -3 to 3
- k_bias: bfloat16 [1024], P('tp'), may hold values from -3 to 3
- v_bias: bfloat16 [1024], P('tp'), may hold values from -3 to 3
- cache_k: bfloat16 [16384, 1024], P('seq', 'tp'), may hold values from -16 to 16
- cache_v: bfloat16 [16384, 1024], P('seq', 'tp'), may hold values from -6 to 6
- deal: int32 [8], replicated, may hold values from 0 to 7, each once
- cache_len: int32 [8], replicated, may hold values from 1 to 2048, 8192 in all
Outputs:
- attn_out: bfloat16 [4096, 8192], P('seq', 'tp')
- new_keys: bfloat16 [4096, 1024], P('seq', 'tp')
- new_values: bfloat16 [4096, 1024], P('seq', 'tp')
- last_norm: float32 [8], P('seq')
- top_logit: float32 [8], P('seq')
The draws below stay inside these ranges and needn't reach their ends.
Inputs may be any that keep to these rules, and one draw needn't show every extreme that they name: `deal`: each request fills exactly one slot. `cache_len`: the lengths sum to 8192 and the largest is exactly 2048.
All inputs are finite; a program needn't handle non-finite values.
Results may differ from the reference program's by a relative error of at most 0.012.
Values may be sent and summed in bfloat16 or wider, within the bound.
No kernel may reach another device: no remote copies, remote signals or barrier semaphores. Data moves between devices by JAX's collectives and lax.ppermute only.
A program may use at most 192 MiB of HBM per device.

```python
import math
import jax
import jax.numpy as jnp
import numpy as np
from jax import lax

HQ = 64
KVH = 8
HEAD = 128
NEW = 512
CACHE = 2048
REQUESTS = 8
TOKENS = 4096
CACHE_ROWS = 16384


def lifted_rows(key, shape):
    return jnp.clip(jax.random.normal(key, shape, jnp.float32), -4.0, 4.0)


def draw_q_new(key, part):
    return lifted_rows(jax.random.fold_in(key, 11), (TOKENS, HQ * HEAD)).astype(jnp.bfloat16)


def draw_cache_k(key, part):
    return lifted_rows(jax.random.fold_in(key, 23), (CACHE_ROWS, KVH * HEAD)).astype(jnp.bfloat16)


def steps_of(own_key, extent, pieces, low, high):
    gain, own = 1.0, jax.random.fold_in(own_key, 6)
    for axis_at, parts in pieces:
        heights = jnp.exp(jax.random.uniform(jax.random.fold_in(own, axis_at), (parts,), jnp.float32, low / len(pieces), high / len(pieces)))
        gain = gain * jnp.repeat(heights, extent[axis_at] // parts).reshape([-1 if axis == axis_at else 1 for axis in range(len(extent))])
    return gain


def profile(amount, total, bound, lean):
    loads = [(1 << 20) // math.isqrt(grade ** lean) + 1 for grade in range(2, amount + 1)]
    rest, counts = total - bound - (amount - 1), [1] * (amount - 1)
    while rest > 0:
        movable = [i for i in range(amount - 1) if counts[i] < bound]
        whole, left = sum([loads[i] for i in movable]), rest
        for i in movable:
            extra = min(bound - counts[i], max(1, left * loads[i] // whole), rest)
            counts[i] = counts[i] + extra
            rest = rest - extra
    return np.array([bound] + counts)


def ragged_sizes(own_key, amount, total, most, skew):
    if amount == 2:
        one = jax.random.randint(own_key, (), max(1, total - most), min(most, total - 1) + 1)
        return jnp.stack([one, total - one])
    tallies = jnp.asarray(profile(amount, total, most, skew), jnp.int32)
    couples = (amount - 1) // 2
    donor, receiver = tallies[1:1 + 2 * couples:2], tallies[2:2 + 2 * couples:2]
    room = jnp.minimum(donor - 1, most - receiver)
    shifted = jax.random.randint(jax.random.fold_in(own_key, 1), (couples,), 0, 1 << 20) % (room + 1)
    tallies = tallies.at[1:1 + 2 * couples:2].set(donor - shifted).at[2:2 + 2 * couples:2].set(receiver + shifted)
    return tallies[jax.random.permutation(jax.random.fold_in(own_key, 2), amount)]


def bell_draw(own_key, dims, width, limit, cuts=(), kind=jnp.bfloat16):
    entries = width * jax.random.normal(own_key, dims, jnp.float32)
    if cuts:
        entries = entries * steps_of(own_key, dims, cuts, -0.22, 0.18)
    return jnp.clip(entries, -limit, limit).astype(kind)


def setup_inputs(seed: int = 0) -> dict:
    seeds = jax.random.split(jax.random.key(seed), 11)
    q_new = draw_q_new(jax.random.fold_in(seeds[10], 71), 0)
    k_new = bell_draw(seeds[1], (TOKENS, KVH * HEAD), 1.0, 6.0, ((0, 8), (1, 4)))
    v_new = bell_draw(seeds[2], (TOKENS, KVH * HEAD), 1.0, 6.0, ((0, 8), (1, 4)))
    q_bias = bell_draw(seeds[3], (HQ * HEAD,), 0.5, 3.0, ((0, 4),))
    k_bias = bell_draw(seeds[4], (KVH * HEAD,), 0.5, 3.0, ((0, 4),))
    v_bias = bell_draw(seeds[5], (KVH * HEAD,), 0.5, 3.0, ((0, 4),))
    cache_k = draw_cache_k(jax.random.fold_in(seeds[10], 71), 0)
    cache_v = bell_draw(seeds[7], (CACHE_ROWS, KVH * HEAD), 1.0, 6.0, ((0, 8), (1, 4)))
    deal = jax.random.permutation(seeds[8], REQUESTS).astype(jnp.int32)
    cache_len = ragged_sizes(seeds[9], REQUESTS, REQUESTS * CACHE // 2, CACHE, 2).astype(jnp.int32)
    return {"q_new": q_new, "k_new": k_new, "v_new": v_new, "q_bias": q_bias, "k_bias": k_bias, "v_bias": v_bias, "cache_k": cache_k, "cache_v": cache_v, "deal": deal, "cache_len": cache_len}


theta_base = 1000000.0

def rotate(vectors, positions):
    half_dim = vectors.shape[-1] // 2
    frequency = theta_base ** (-2.0 * jnp.arange(half_dim, dtype=jnp.float32) / vectors.shape[-1])
    angles = positions.astype(jnp.float32)[:, None] * frequency[None, :]
    cosine = jnp.cos(angles)[:, None, :]
    sine_part = jnp.sin(angles)[:, None, :]
    lower_part = vectors[..., :half_dim]
    upper_part = vectors[..., half_dim:]
    return jnp.concatenate([lower_part * cosine - upper_part * sine_part, upper_part * cosine + lower_part * sine_part], axis=-1)

def reference(q_new, k_new, v_new, q_bias, k_bias, v_bias, cache_k, cache_v, deal, cache_len):
    group = HQ // KVH
    slot_ids = jnp.arange(REQUESTS, dtype=jnp.int32)
    inverse = lax.optimization_barrier(jnp.sum(jnp.where(deal[None, :] == slot_ids[:, None], slot_ids[None, :], 0), axis=1)).astype(jnp.int32)
    q_req = jnp.take(q_new.reshape(REQUESTS, NEW, HQ * HEAD), inverse, axis=0)
    k_req = jnp.take(k_new.reshape(REQUESTS, NEW, KVH * HEAD), inverse, axis=0)
    v_req = jnp.take(v_new.reshape(REQUESTS, NEW, KVH * HEAD), inverse, axis=0)

    def one_request(item):
        q_raw, k_raw, v_raw, stored_k, stored_v, length = item
        positions = length + jnp.arange(NEW, dtype=jnp.int32)
        queries = rotate((q_raw.astype(jnp.float32) + q_bias.astype(jnp.float32)).reshape(NEW, HQ, HEAD), positions).astype(jnp.bfloat16)
        fresh_keys = rotate((k_raw.astype(jnp.float32) + k_bias.astype(jnp.float32)).reshape(NEW, KVH, HEAD), positions).astype(jnp.bfloat16)
        fresh_values = (v_raw.astype(jnp.float32) + v_bias.astype(jnp.float32)).astype(jnp.bfloat16).reshape(NEW, KVH, HEAD)
        key_rows = jnp.concatenate([stored_k.reshape(CACHE, KVH, HEAD), fresh_keys], axis=0).astype(jnp.float32)
        value_rows = jnp.concatenate([stored_v.reshape(CACHE, KVH, HEAD), fresh_values], axis=0).astype(jnp.float32)
        grouped = queries.reshape(NEW, KVH, group, HEAD).astype(jnp.float32)
        scores = jnp.einsum('qkgd,tkd->kgqt', grouped, key_rows) * HEAD ** (-0.5)
        row_ids = jnp.arange(NEW, dtype=jnp.int32)[:, None]
        col_ids = jnp.arange(CACHE + NEW, dtype=jnp.int32)[None, :]
        valid = (col_ids < length) | (col_ids >= CACHE) & (col_ids - CACHE <= row_ids)
        scores = jnp.where(valid, scores, -jnp.inf)
        running_max = lax.optimization_barrier(jnp.max(scores, axis=-1))
        weight = jnp.exp(scores - running_max[..., None])
        row_total = lax.optimization_barrier(jnp.sum(weight, axis=-1))
        rounded = lax.optimization_barrier(weight.astype(jnp.bfloat16)).astype(jnp.float32)
        weighted = jnp.einsum('kgqt,tkd->kgqd', rounded, value_rows)
        mixture = (weighted / row_total[..., None]).transpose(2, 0, 1, 3).reshape(NEW, HQ * HEAD)
        last_row = mixture[NEW - 1]
        norm_value = jnp.sqrt(jnp.mean(last_row * last_row) + 1e-06)
        top_value = jnp.max(running_max[:, :, NEW - 1])
        return (mixture.astype(jnp.bfloat16), fresh_keys.reshape(NEW, KVH * HEAD), fresh_values.reshape(NEW, KVH * HEAD), norm_value, top_value)
    results = lax.map(one_request, (q_req, k_req, v_req, cache_k.reshape(REQUESTS, CACHE, KVH * HEAD), cache_v.reshape(REQUESTS, CACHE, KVH * HEAD), cache_len))
    return (results[0].reshape(TOKENS, HQ * HEAD), results[1].reshape(TOKENS, KVH * HEAD), results[2].reshape(TOKENS, KVH * HEAD), results[3], results[4])
```

```python
import functools
import itertools
import math

import jax
import jax.numpy as jnp
import numpy as np
from jax import lax
from jax.experimental import pallas as pl
from jax.experimental.pallas import tpu as pltpu
from jax.sharding import PartitionSpec as P

HEAD = 128
LOG2E = 1.4426950408889634
theta_base = 1000000.0
masked_score = -1e30
norm_epsilon = 1e-06
f32, bf16 = jnp.float32, jnp.bfloat16

SAFE = 60.0
ROWS_T = (((1,), (1,)), ((), ()))
PLAIN = (((1,), (0,)), ((), ()))

def fold(x):
    part = x[:, :HEAD]
    for j in range(1, x.shape[1] // HEAD):
        part = part + x[:, j * HEAD : (j + 1) * HEAD]
    return part

def twice(x):
    return jnp.concatenate([x, x], axis=1)

def attend_kernel(
    meta, q1, q2, qb, q_bias, cos, sin, ck, cv, nk, nv, norms,
    o_ref, stat,
    qs, kblk, vblk, m_s, l_s, acc,
    *, skip, first, rows, group, block, tail,
):
    length, side, by_first = meta[0], meta[1], meta[2] != 0
    half = rows // 2
    scale = HEAD**-0.5 * LOG2E
    body = slice(skip, skip + half)
    for mine, turn in ((True, side), (False, 1 - side)):
        spot = pl.multiple_of(turn * half, half)
        here = pl.ds(pl.multiple_of(spot + first, 16), half)
        c, s = cos[here, :], sin[here, :]
        for h in range(group):
            column = slice(h * HEAD, (h + 1) * HEAD)
            if mine:
                raw = jnp.where(by_first, q1[body, column].astype(f32), q2[body, column].astype(f32))
            else:
                raw = qb[body, column].astype(f32)
            x = raw + q_bias[:, column].astype(f32)
            y = (x * c + pltpu.roll(x, HEAD // 2, 1) * s).astype(bf16).astype(f32)
            z = y * scale
            high = z.astype(bf16)
            at = pl.ds(pl.multiple_of(h * rows + spot, 16), half)
            qs[at, :HEAD] = high
            qs[at, HEAD:] = (z - high.astype(f32)).astype(bf16)
    high = qs[:, :HEAD].astype(f32)
    lengths = lax.dot_general(
        (high * high).astype(bf16), jnp.ones((HEAD, HEAD), bf16), PLAIN, preferred_element_type=f32
    )
    biggest = jnp.max(lengths.reshape(group * rows // 8, 8, HEAD), axis=0)
    bound = jnp.max(biggest) * jnp.max(norms[...])
    l_s[...] = jnp.zeros(l_s.shape, f32)
    acc[...] = jnp.zeros(acc.shape, f32)
    full = length // block
    cached = (length + block - 1) // block
    newer = (first + rows + block - 1) // block

    def load(i):
        is_new = i >= cached
        at = pl.multiple_of(jnp.where(is_new, i - cached, i) * block, block)

        @pl.when(is_new)
        def _():
            kblk[...] = nk[pl.ds(at, block), :]
            vblk[...] = nv[pl.ds(at, block), :]

        @pl.when(jnp.logical_not(is_new))
        def _():
            kblk[...] = ck[pl.ds(at, block), :]
            vblk[...] = cv[pl.ds(at, block), :]

        return jnp.where(is_new, first + 1, length) - at, jnp.where(is_new, 1, 0)

    def allowed(shape, base, limit, slope):
        row = (lax.broadcasted_iota(jnp.int32, (shape[0], 1), 0) + base) % rows
        return lax.broadcasted_iota(jnp.int32, shape, 1) < limit + slope * row

    @pl.when(bound <= SAFE * SAFE)
    def _():
        def add(k, v, valid):
            weight = jnp.exp2(lax.dot_general(qs[...], twice(k), ROWS_T, preferred_element_type=f32))
            if valid is not None:
                weight = jnp.where(valid(weight.shape), weight, 0.0)
            l_s[...] += fold(weight)
            acc[...] += lax.dot_general(weight.astype(bf16), v, PLAIN, preferred_element_type=f32)

        def whole(i, carry):
            at = pl.ds(pl.multiple_of(i * block, block), block)
            add(ck[at, :], cv[at, :], None)
            return carry

        def partial(i, carry):
            limit, slope = load(i)
            add(kblk[...], vblk[...], lambda shape: allowed(shape, 0, limit, slope))
            return carry

        lax.fori_loop(0, full, whole, 0)
        lax.fori_loop(full, cached + newer, partial, 0)

    @pl.when(bound > SAFE * SAFE)
    def _():
        m_s[...] = jnp.full(m_s.shape, masked_score, f32)

        def online(i, carry):
            limit, slope = load(i)

            def piece(h, carry):
                at = pl.ds(pl.multiple_of(h * rows, 16), rows)
                scores = lax.dot_general(qs[at, :], twice(kblk[...]), ROWS_T, preferred_element_type=f32)
                scores = jnp.where(allowed(scores.shape, 0, limit, slope), scores, masked_score)
                old = m_s[at, :]
                new = jnp.maximum(old, jnp.max(scores, axis=1, keepdims=True))
                m_s[at, :] = new
                weight = jnp.exp2(scores - jnp.tile(new, (1, block // HEAD)))
                factor = jnp.exp2(old - new)
                l_s[at, :] = l_s[at, :] * factor + fold(weight)
                acc[at, :] = acc[at, :] * factor + lax.dot_general(
                    weight.astype(bf16), vblk[...], PLAIN, preferred_element_type=f32
                )
                return carry

            return lax.fori_loop(0, group, piece, carry)

        lax.fori_loop(0, cached + newer, online, 0)

    squares = jnp.zeros((8, HEAD), f32)
    for h in range(group):
        at = slice(h * rows, (h + 1) * rows)
        mixture = acc[at, :] / jnp.sum(l_s[at, :], axis=1, keepdims=True)
        o_ref[:, h * HEAD : (h + 1) * HEAD] = mixture.astype(bf16)
        end = mixture[rows - 8 :, :]
        squares = squares + end * end
    if tail:
        last = jnp.concatenate([qs[h * rows + rows - 16 : (h + 1) * rows, :] for h in range(group)], axis=0)

        def highest(i, top):
            limit, slope = load(i)
            scores = lax.dot_general(twice(kblk[...]), last, ROWS_T, preferred_element_type=f32)
            key = lax.broadcasted_iota(jnp.int32, scores.shape, 0)
            scores = jnp.where(key < limit + slope * (rows - 1), scores, masked_score)
            return jnp.maximum(top, jnp.max(scores.reshape(block // 8, 8, group * 16), axis=0))

        top = lax.fori_loop(0, cached + newer, highest, jnp.full((8, group * 16), masked_score, f32))
        lane = lax.broadcasted_iota(jnp.int32, top.shape, 1)
        top = jnp.where(lane % 16 == 15, top, masked_score)
        stat[0:8, :] = squares
        stat[8:16, :] = jnp.max(top, axis=(0, 1), keepdims=True) * (1.0 / LOG2E) + jnp.zeros((8, HEAD), f32)
    else:
        stat[...] = jnp.zeros_like(stat)

def attend(meta, arrived, bias, angles, caches, news, norms, skip, first, tail, kv_heads, block):
    height, q_cols = arrived[0].shape
    half = height - skip
    rows = 2 * half
    group = q_cols // HEAD // kv_heads
    wide = group * HEAD
    fresh, cache_rows = news[0].shape[0], caches[0].shape[0]
    column = lambda n, width: pl.BlockSpec((n, width), lambda g, m: (0, g))
    table = pl.BlockSpec((fresh, HEAD), lambda g, m: (0, 0))
    spec = pltpu.PrefetchScalarGridSpec(
        num_scalar_prefetch=1, grid=(kv_heads,),
        in_specs=[
            column(height, wide), column(height, wide), column(height, wide), column(1, wide), table, table,
            column(cache_rows, HEAD), column(cache_rows, HEAD), column(fresh, HEAD), column(fresh, HEAD), column(8, HEAD),
        ],
        out_specs=[column(rows, wide), column(16, HEAD)],
        scratch_shapes=[
            pltpu.VMEM((group * rows, 2 * HEAD), bf16), pltpu.VMEM((block, HEAD), bf16), pltpu.VMEM((block, HEAD), bf16),
            pltpu.VMEM((group * rows, HEAD), f32), pltpu.VMEM((group * rows, HEAD), f32), pltpu.VMEM((group * rows, HEAD), f32),
        ],
    )
    work = kv_heads * group * rows * (cache_rows // 2 + fresh)
    return pl.pallas_call(
        functools.partial(attend_kernel, skip=skip, first=first, rows=rows, group=group, block=block, tail=tail),
        grid_spec=spec,
        out_shape=[jax.ShapeDtypeStruct((rows, q_cols), bf16), jax.ShapeDtypeStruct((16, kv_heads * HEAD), f32)],
        compiler_params=pltpu.CompilerParams(vmem_limit_bytes=48 << 20),
        cost_estimate=pl.CostEstimate(flops=4 * work * HEAD, bytes_accessed=4 * cache_rows * HEAD * kv_heads, transcendentals=work),
        name="attend",
    )(meta, *arrived, bias, *angles, *caches, *news, norms)


def tables(length, rows):
    half = HEAD // 2
    frequency = theta_base ** (-2.0 * jnp.arange(half, dtype=f32) / HEAD)
    positions = length + jnp.arange(rows, dtype=jnp.int32)
    angles = positions.astype(f32)[:, None] * frequency[None, :]
    cosine, sine = jnp.cos(angles), jnp.sin(angles)
    return jnp.concatenate([cosine, cosine], 1), jnp.concatenate([-sine, sine], 1)


def longest(keys, valid):
    wide = keys.astype(f32)
    squares = (wide * wide).astype(bf16)
    sums = lax.dot_general(squares, jnp.ones((HEAD, HEAD), bf16), PLAIN, preferred_element_type=f32)
    if valid is not None:
        sums = jnp.where(lax.broadcasted_iota(jnp.int32, sums.shape, 0) < valid, sums, 0.0)
    return jnp.max(sums.reshape(sums.shape[0] // 8, 8, HEAD), axis=0) * 1.05


def fresh_kernel(meta, x1, x2, xb, k_bias, v_bias, cos, sin, ck, k_out, v_out, norms, *, half, packs):
    length, side, by_first = meta[0], meta[1], meta[2] != 0
    cols = k_out.shape[1]
    for mine, turn in ((True, side), (False, 1 - side)):
        for j in range(packs):
            here = pl.ds(pl.multiple_of(2 * half * j + turn * half, half), half)
            pack = slice(2 * cols * j, 2 * cols * (j + 1))
            if mine:
                raw = jnp.where(by_first, x1[:half, pack].astype(f32), x2[:half, pack].astype(f32))
            else:
                raw = xb[:half, pack].astype(f32)
            c, s = cos[here, :], sin[here, :]
            for h in range(cols // HEAD):
                column = slice(h * HEAD, (h + 1) * HEAD)
                x = raw[:, column] + k_bias[:, column].astype(f32)
                k_out[here, column] = (x * c + pltpu.roll(x, HEAD // 2, 1) * s).astype(bf16)
            v_out[here, :] = (raw[:, cols:] + v_bias[...].astype(f32)).astype(bf16)
    for h in range(cols // HEAD):
        column = slice(h * HEAD, (h + 1) * HEAD)
        norms[:, column] = jnp.maximum(longest(k_out[:, column], None), longest(ck[:, column], length))


def fresh_rows(meta, arrived, k_bias, v_bias, angles, cache_k, total):
    cols = k_bias.shape[1]
    packs = arrived[0].shape[1] // (2 * cols)
    whole = pl.BlockSpec(memory_space=pltpu.VMEM)
    return pl.pallas_call(
        functools.partial(fresh_kernel, half=total // packs // 2, packs=packs),
        in_specs=[pl.BlockSpec(memory_space=pltpu.SMEM)] + [whole] * 8,
        out_specs=[whole] * 3,
        out_shape=[
            jax.ShapeDtypeStruct((total, cols), bf16),
            jax.ShapeDtypeStruct((total, cols), bf16),
            jax.ShapeDtypeStruct((8, cols), f32),
        ],
        compiler_params=pltpu.CompilerParams(vmem_limit_bytes=32 << 20),
        name="fresh",
    )(meta, *arrived, k_bias, v_bias, *angles, cache_k)


def summary(stat):
    squares = jnp.sum(stat[7, :])
    top = jnp.max(stat[15, :])
    size = lax.axis_size("tp")
    pair = jnp.stack([squares, top]).reshape(1, 2)
    step = 1
    while step < size:
        other = lax.ppermute(pair, "tp", [(i, i ^ step) for i in range(size)])
        pair = jnp.concatenate([pair[:, :1] + other[:, :1], jnp.maximum(pair[:, 1:], other[:, 1:])], 1)
        step *= 2
    return pair[0, 0], pair[0, 1]


LINE = 4
Z_PERMS = list(itertools.permutations(range(LINE)))


def z_pairs(perm):
    return [(2 * z + y, 2 * perm[z] + y) for z in range(LINE) for y in range(2)]


def z_load(perm):
    up = [sum(1 for z in range(LINE) if z <= k < perm[z]) for k in range(LINE - 1)]
    down = [sum(1 for z in range(LINE) if perm[z] <= k < z) for k in range(LINE - 1)]
    return max(up + down)


def plan(deal, own):
    bits = np.array(list(itertools.product((0, 1), repeat=LINE)), np.int32)
    perms = np.array(Z_PERMS, np.int32)
    loads = np.array([z_load(p) for p in Z_PERMS], np.int32)
    place = deal.reshape(LINE, 2) // 2
    first = jnp.where(bits == 0, place[None, :, 0], place[None, :, 1])
    second = jnp.sum(place, axis=1)[None, :] - first
    same_1 = jnp.all(first[:, None, :] == perms[None], axis=2)
    same_2 = jnp.all(second[:, None, :] == perms[None], axis=2)
    number = np.arange(len(Z_PERMS), dtype=np.int32)
    index_1 = jnp.sum(jnp.where(same_1, number, 0), axis=1)
    index_2 = jnp.sum(jnp.where(same_2, number, 0), axis=1)
    cost = jnp.sum(jnp.where(same_1, loads, 0), axis=1) + jnp.sum(jnp.where(same_2, loads, 0), axis=1)
    legal = jnp.any(same_1, axis=1) & jnp.any(same_2, axis=1)
    ticket = jnp.where(legal, cost, 99) * len(bits) + np.arange(len(bits), dtype=np.int32)
    chosen = ticket == jnp.min(ticket)
    pick = lambda values: jnp.sum(jnp.where(chosen, values, 0))
    bit = jnp.sum(jnp.where(chosen[:, None], bits, 0), axis=0)
    slot = np.arange(2 * LINE, dtype=np.int32)
    by_first = jnp.repeat(bit, 2) == slot % 2
    mine_first = jnp.any((deal == own) & by_first)
    leaves_first = jnp.sum(jnp.where(np.arange(LINE) == own // 2, bit, 0))
    return pick(index_1), pick(index_2), leaves_first, mine_first


def cut_rows(total):
    unit = total // 16
    return [3 * unit, 7 * unit, 6 * unit]


def body(q_new, k_new, v_new, q_bias, k_bias, v_bias, cache_k, cache_v, deal, cache_len):
    slots = lax.axis_size("seq")
    own = lax.axis_index("seq").astype(jnp.int32)
    slot_ids = jnp.arange(slots, dtype=jnp.int32)
    length = jnp.sum(jnp.where(slot_ids == own, cache_len, 0))
    total, q_cols = q_new.shape
    kv_cols = k_new.shape[1]
    kv_heads = kv_cols // HEAD
    block = math.gcd(512, cache_k.shape[0], total)
    q_bias, k_bias, v_bias = (x.reshape(1, -1) for x in (q_bias, k_bias, v_bias))
    angles = tables(length, total)
    caches = (cache_k, cache_v)
    packs = q_cols // (2 * kv_cols)
    kv_half = total // packs // 2
    sizes = cut_rows(total)
    firsts = [total - sum(sizes[: i + 1]) for i in range(len(sizes))]

    def kv_rows(h):
        return [x[(2 * j + h) * kv_half : (2 * j + h + 1) * kv_half] for j in range(packs) for x in (k_new, v_new)]

    def q_rows(i, h):
        half = sizes[i] // 2
        return q_new[firsts[i] + h * half : firsts[i] + (h + 1) * half]

    def chunk_half(i, h):
        if i:
            return q_rows(i, h)
        return jnp.concatenate([jnp.concatenate(kv_rows(h), axis=1), q_rows(0, h)], axis=0)

    if slots == 2 * LINE:
        side = own % 2
        route_1, route_2, leaves_first, mine_first = plan(deal, own)
        swap = [(i, i ^ 1) for i in range(slots)]
        own_first = leaves_first == side

        def hop(route, piece):
            branches = [functools.partial(lax.ppermute, axis_name="seq", perm=z_pairs(p)) for p in Z_PERMS]
            return lax.switch(route, branches, piece)

        kept, received = [], []
        for i in range(len(sizes)):
            a, b = chunk_half(i, 0), chunk_half(i, 1)
            kept.append(jnp.where(side == 0, a, b))
            received.append(lax.ppermute(jnp.where(side == 0, b, a), "seq", swap))
        arrived = []
        for keep, recv in zip(kept, received):
            moved_1 = hop(route_1, jnp.where(own_first, keep, recv))
            moved_2 = hop(route_2, jnp.where(own_first, recv, keep))
            got = lax.ppermute(jnp.where(mine_first, moved_2, moved_1), "seq", swap)
            arrived.append((moved_1, moved_2, got))
        meta = jnp.stack([length, side, mine_first.astype(jnp.int32)])
        meta, _ = lax.optimization_barrier((meta, arrived[-1][1]))
    else:
        inverse = jnp.sum(jnp.where(deal[None, :] == slot_ids[:, None], slot_ids[None, :], 0), axis=1)

        def settle(x):
            spread = lax.all_to_all(x.reshape(slots, -1, x.shape[1]), "seq", split_axis=0, concat_axis=0, tiled=True)
            picked = jnp.take(spread, inverse, axis=0)
            return lax.all_to_all(picked, "seq", split_axis=0, concat_axis=0, tiled=True).reshape(x.shape)

        arrived = []
        whole = settle(jnp.concatenate([jnp.concatenate([chunk_half(i, h) for h in range(2)]) for i in range(len(sizes))]))
        at = 0
        for i in range(len(sizes)):
            half = sizes[i] // 2 + (0 if i else kv_half)
            arrived.append((whole[at : at + half], whole[at : at + half], whole[at + half : at + 2 * half]))
            at += 2 * half
        meta = jnp.stack([length, jnp.int32(0), jnp.int32(1)])
    new_k, new_v, norms = fresh_rows(meta, arrived[0], k_bias, v_bias, angles, cache_k, total)
    parts = []
    for i in range(len(sizes)):
        part, stat = attend(
            meta, arrived[i], q_bias, angles, caches, (new_k, new_v), norms,
            0 if i else kv_half, firsts[i], i == 0, kv_heads, block,
        )
        parts.append(part)
        if i == 0:
            squares, top = summary(stat)
    out = jnp.concatenate(parts[::-1], axis=0)
    features = q_cols * lax.axis_size("tp")
    norm = jnp.sqrt(squares / features + norm_epsilon)
    return out, new_k, new_v, norm.reshape(1), top.reshape(1)


def solution(mesh):
    return jax.shard_map(
        body,
        mesh=mesh,
        in_specs=(
            P("seq", "tp"),
            P("seq", "tp"),
            P("seq", "tp"),
            P("tp"),
            P("tp"),
            P("tp"),
            P("seq", "tp"),
            P("seq", "tp"),
            P(),
            P(),
        ),
        out_specs=(P("seq", "tp"), P("seq", "tp"), P("seq", "tp"), P("seq"), P("seq")),
        check_vma=False,
    )
```

```python
import functools
import math

import jax
import jax.numpy as jnp
from jax import lax
from jax.experimental import pallas as pl
from jax.experimental.pallas import tpu as pltpu
from jax.sharding import PartitionSpec as P

HEAD = 128
LOG2E = 1.4426950408889634
theta_base = 1000000.0
masked_score = -1e30
norm_epsilon = 1e-06
f32, bf16 = jnp.float32, jnp.bfloat16

SAFE = 60.0
ROWS_T = (((1,), (1,)), ((), ()))
PLAIN = (((1,), (0,)), ((), ()))
ANY = pl.BlockSpec(memory_space=pl.ANY)
SMEM = pl.BlockSpec(memory_space=pltpu.SMEM)


def fold(x):
    part = x[:, :HEAD]
    for j in range(1, x.shape[1] // HEAD):
        part = part + x[:, j * HEAD : (j + 1) * HEAD]
    return part


def twice(x):
    return jnp.concatenate([x, x], axis=1)


def attend_kernel(*refs, skip, offset, size, period, group, wide_block, block, tail):
    meta, arrived, q_bias, cos, sin, ck, cv, nk, nv, norms = refs[:10]
    o_ref, stat, qs, m_s, l_s, acc = refs[-6:]
    length = meta[0]
    scale = HEAD**-0.5 * LOG2E
    pieces = arrived.shape[0]
    rows = pieces * size
    for e in range(pieces):
        here = slice(e * period + offset, e * period + offset + size)
        c, s = cos[here, :], sin[here, :]
        for h in range(group):
            column = slice(h * HEAD, (h + 1) * HEAD)
            x = arrived[e, skip : skip + size, column].astype(f32) + q_bias[:, column].astype(f32)
            y = (x * c + pltpu.roll(x, HEAD // 2, 1) * s).astype(bf16).astype(f32)
            z = y * scale
            high = z.astype(bf16)
            at = slice(h * rows + e * size, h * rows + (e + 1) * size)
            qs[at, :HEAD] = high
            qs[at, HEAD:] = (z - high.astype(f32)).astype(bf16)
    high = qs[:, :HEAD].astype(f32)
    lengths = lax.dot_general(
        (high * high).astype(bf16), jnp.ones((HEAD, HEAD), bf16), PLAIN, preferred_element_type=f32
    )
    biggest = jnp.max(lengths.reshape(group * rows // 8, 8, HEAD), axis=0)
    bound = jnp.max(biggest) * jnp.max(norms[...])
    l_s[...] = jnp.zeros(l_s.shape, f32)
    acc[...] = jnp.zeros(acc.shape, f32)
    whole = length // wide_block
    rest = whole * (wide_block // block)
    cached = (length + block - 1) // block

    def causal(heads, width):
        shape = (heads * pieces, size, width)
        piece = lax.broadcasted_iota(jnp.int32, shape, 0) % pieces
        row = (piece * period + lax.broadcasted_iota(jnp.int32, shape, 1)).reshape(heads * rows, width)
        return lax.broadcasted_iota(jnp.int32, (heads * rows, width), 1) - row <= offset

    @pl.when(bound <= SAFE * SAFE)
    def _():
        def add(k, v, valid):
            weight = jnp.exp2(lax.dot_general(qs[...], twice(k), ROWS_T, preferred_element_type=f32))
            if valid is not None:
                weight = jnp.where(valid, weight, 0.0)
            l_s[...] += fold(weight)
            acc[...] += lax.dot_general(weight.astype(bf16), v, PLAIN, preferred_element_type=f32)

        def full(i, carry):
            at = pl.ds(pl.multiple_of(i * wide_block, wide_block), wide_block)
            add(ck[at, :], cv[at, :], None)
            return carry

        def partial(i, carry):
            at = pl.ds(pl.multiple_of(i * block, block), block)
            key = lax.broadcasted_iota(jnp.int32, (group * rows, block), 1)
            add(ck[at, :], cv[at, :], key < length - i * block)
            return carry

        lax.fori_loop(0, whole, full, 0)
        lax.fori_loop(rest, cached, partial, 0)
        add(nk[...], nv[...], causal(group, nk.shape[0]))

    @pl.when(bound > SAFE * SAFE)
    def _():
        m_s[...] = jnp.full(m_s.shape, masked_score, f32)

        def online(k, v, valid):
            def piece(h, carry):
                at = pl.ds(pl.multiple_of(h * rows, 16), rows)
                scores = lax.dot_general(qs[at, :], twice(k), ROWS_T, preferred_element_type=f32)
                scores = jnp.where(valid, scores, masked_score)
                old = m_s[at, :]
                new = jnp.maximum(old, jnp.max(scores, axis=1, keepdims=True))
                m_s[at, :] = new
                weight = jnp.exp2(scores - jnp.tile(new, (1, k.shape[0] // HEAD)))
                factor = jnp.exp2(old - new)
                l_s[at, :] = l_s[at, :] * factor + fold(weight)
                acc[at, :] = acc[at, :] * factor + lax.dot_general(
                    weight.astype(bf16), v, PLAIN, preferred_element_type=f32
                )
                return carry

            lax.fori_loop(0, group, piece, 0)

        def step(i, carry):
            at = pl.ds(pl.multiple_of(i * block, block), block)
            key = lax.broadcasted_iota(jnp.int32, (rows, block), 1)
            online(ck[at, :], cv[at, :], key < length - i * block)
            return carry

        lax.fori_loop(0, cached, step, 0)
        online(nk[...], nv[...], causal(1, nk.shape[0]))

    squares = jnp.zeros((8, HEAD), f32)
    for h in range(group):
        at = slice(h * rows, (h + 1) * rows)
        mixture = acc[at, :] / jnp.sum(l_s[at, :], axis=1, keepdims=True)
        o_ref[:, :, h * HEAD : (h + 1) * HEAD] = mixture.astype(bf16).reshape(pieces, size, HEAD)
        end = mixture[rows - 8 :, :]
        squares = squares + end * end
    if tail:
        last = jnp.concatenate([qs[(h + 1) * rows - 16 : (h + 1) * rows, :] for h in range(group)], axis=0)
        old_scores = lax.dot_general(twice(ck[...]), last, ROWS_T, preferred_element_type=f32)
        key = lax.broadcasted_iota(jnp.int32, old_scores.shape, 0)
        old_scores = jnp.where(key < length, old_scores, masked_score)
        new_scores = lax.dot_general(twice(nk[...]), last, ROWS_T, preferred_element_type=f32)
        top = jnp.maximum(
            jnp.max(old_scores.reshape(-1, 8, group * 16), axis=0),
            jnp.max(new_scores.reshape(-1, 8, group * 16), axis=0),
        )
        lane = lax.broadcasted_iota(jnp.int32, top.shape, 1)
        top = jnp.where(lane % 16 == 15, top, masked_score)
        stat[0:8, :] = squares
        stat[8:16, :] = jnp.max(top, axis=(0, 1), keepdims=True) * (1.0 / LOG2E) + jnp.zeros((8, HEAD), f32)
    else:
        stat[...] = jnp.zeros_like(stat)


def attend(meta, arrived, bias, angles, caches, news, norms, out, offset, size, tail, kv_heads):
    pieces, height, q_cols = arrived.shape
    rows = pieces * size
    group = q_cols // HEAD // kv_heads
    wide = group * HEAD
    fresh, cache_rows = news[0].shape[0], caches[0].shape[0]
    period = fresh // pieces
    wide_block, block = math.gcd(1024, cache_rows), math.gcd(512, cache_rows)
    column = lambda n, width: pl.BlockSpec((n, width), lambda g, m: (0, g))
    table = pl.BlockSpec((fresh, HEAD), lambda g, m: (0, 0))
    given = [] if out is None else [out]
    spec = pltpu.PrefetchScalarGridSpec(
        num_scalar_prefetch=1,
        grid=(kv_heads,),
        in_specs=[
            pl.BlockSpec((pieces, height, wide), lambda g, m: (0, 0, g)), column(1, wide), table, table,
            column(cache_rows, HEAD), column(cache_rows, HEAD), column(fresh, HEAD), column(fresh, HEAD), column(8, HEAD),
        ] + [ANY] * len(given),
        out_specs=[pl.BlockSpec((pieces, size, wide), lambda g, m: (0, offset // size, g)), column(16, HEAD)],
        scratch_shapes=[
            pltpu.VMEM((group * rows, 2 * HEAD), bf16),
            pltpu.VMEM((group * rows, HEAD), f32),
            pltpu.VMEM((group * rows, HEAD), f32),
            pltpu.VMEM((group * rows, HEAD), f32),
        ],
    )
    work = kv_heads * group * rows * (cache_rows // 2 + fresh)
    return pl.pallas_call(
        functools.partial(
            attend_kernel, skip=height - size, offset=offset, size=size, period=period, group=group,
            wide_block=wide_block, block=block, tail=tail,
        ),
        grid_spec=spec,
        out_shape=[
            jax.ShapeDtypeStruct((pieces, period, q_cols), bf16),
            jax.ShapeDtypeStruct((16, kv_heads * HEAD), f32),
        ],
        input_output_aliases={10: 0} if given else {},
        compiler_params=pltpu.CompilerParams(vmem_limit_bytes=60 << 20),
        cost_estimate=pl.CostEstimate(
            flops=4 * work * HEAD, bytes_accessed=4 * cache_rows * HEAD * kv_heads, transcendentals=work
        ),
        name="attend",
    )(meta, arrived, bias, *angles, *caches, *news, norms, *given)


def tables(length, rows):
    half = HEAD // 2
    frequency = theta_base ** (-2.0 * jnp.arange(half, dtype=f32) / HEAD)
    positions = length + jnp.arange(rows, dtype=jnp.int32)
    angles = positions.astype(f32)[:, None] * frequency[None, :]
    cosine, sine = jnp.cos(angles), jnp.sin(angles)
    return jnp.concatenate([cosine, cosine], 1), jnp.concatenate([-sine, sine], 1)


def longest(keys, valid):
    wide = keys.astype(f32)
    squares = (wide * wide).astype(bf16)
    sums = lax.dot_general(squares, jnp.ones((HEAD, HEAD), bf16), PLAIN, preferred_element_type=f32)
    if valid is not None:
        sums = jnp.where(lax.broadcasted_iota(jnp.int32, sums.shape, 0) < valid, sums, 0.0)
    return jnp.max(sums.reshape(sums.shape[0] // 8, 8, HEAD), axis=0) * 1.05


def fresh_kernel(meta, arrived, k_bias, v_bias, cos, sin, ck, k_out, v_out, norms, *, size, packs):
    length = meta[0]
    cols = k_out.shape[1]
    for e in range(arrived.shape[0]):
        for b in range(packs):
            here = slice((e * packs + b) * size, (e * packs + b + 1) * size)
            raw = arrived[e, :size, 2 * cols * b : 2 * cols * (b + 1)].astype(f32)
            c, s = cos[here, :], sin[here, :]
            for h in range(cols // HEAD):
                column = slice(h * HEAD, (h + 1) * HEAD)
                x = raw[:, column] + k_bias[:, column].astype(f32)
                k_out[here, column] = (x * c + pltpu.roll(x, HEAD // 2, 1) * s).astype(bf16)
            v_out[here, :] = (raw[:, cols:] + v_bias[...].astype(f32)).astype(bf16)
    for h in range(cols // HEAD):
        column = slice(h * HEAD, (h + 1) * HEAD)
        norms[:, column] = jnp.maximum(longest(k_out[:, column], None), longest(ck[:, column], length))


def fresh_rows(meta, arrived, k_bias, v_bias, angles, cache_k, size):
    pieces, _, width = arrived.shape
    cols = k_bias.shape[1]
    packs = width // (2 * cols)
    total = pieces * packs * size
    whole = pl.BlockSpec(memory_space=pltpu.VMEM)
    return pl.pallas_call(
        functools.partial(fresh_kernel, size=size, packs=packs),
        in_specs=[SMEM] + [whole] * 6,
        out_specs=[whole] * 3,
        out_shape=[
            jax.ShapeDtypeStruct((total, cols), bf16),
            jax.ShapeDtypeStruct((total, cols), bf16),
            jax.ShapeDtypeStruct((8, cols), f32),
        ],
        compiler_params=pltpu.CompilerParams(vmem_limit_bytes=32 << 20),
        name="fresh",
    )(meta, arrived, k_bias, v_bias, *angles, cache_k)


def swap_tp(pair, step):
    size = lax.axis_size("tp")
    return lax.ppermute(pair, "tp", [(i, i ^ step) for i in range(size)])


def run_copies(copies):
    for copy in copies:
        copy.start()
    for copy in copies:
        copy.wait()


def deal_kernel(q, k, v, out, held, sems, *, packs):
    pieces, height, _ = held.shape
    size = q.shape[0] // pieces
    kv_size = height - size
    copies = []
    for e in range(pieces):
        copies.append((q.at[pl.ds(e * size, size)], held.at[e, pl.ds(kv_size, size)]))
        for b in range(packs):
            rows = pl.ds((e * packs + b) * kv_size, kv_size)
            for n, x in enumerate((k, v)):
                width = x.shape[1]
                copies.append((x.at[rows], held.at[e, pl.ds(0, kv_size), pl.ds((2 * b + n) * width, width)]))
    run_copies([pltpu.make_async_copy(a, b, sems.at[n]) for n, (a, b) in enumerate(copies)])
    run_copies([pltpu.make_async_copy(held, out, sems.at[0])])


def deal_pieces(q, k, v, pieces, packs):
    total, q_cols = q.shape
    shape = (pieces, total // pieces + total // pieces // packs, q_cols)
    return pl.pallas_call(
        functools.partial(deal_kernel, packs=packs),
        in_specs=[ANY] * 3,
        out_specs=ANY,
        out_shape=jax.ShapeDtypeStruct(shape, bf16),
        scratch_shapes=[pltpu.VMEM(shape, bf16), pltpu.SemaphoreType.DMA((pieces * (1 + 2 * packs),))],
        compiler_params=pltpu.CompilerParams(vmem_limit_bytes=60 << 20),
        name="deal",
    )(q, k, v)


def route_kernel(deal, x, out, held, sems, *, spans):
    slots = x.shape[0]
    into, back = [], []
    for s in range(slots):
        base = 0
        for n, (offset, size) in enumerate(spans):
            into.append(pltpu.make_async_copy(x.at[s, pl.ds(offset, size)], held.at[s, pl.ds(base, size)], sems.at[n, s]))
            base += size
        back.append(pltpu.make_async_copy(held.at[s], out.at[deal[s]], sems.at[0, s]))
    run_copies(into)
    run_copies(back)


def route(deal, x, spans):
    slots, _, q_cols = x.shape
    shape = (slots, sum(size for _, size in spans), q_cols)
    return pl.pallas_call(
        functools.partial(route_kernel, spans=spans),
        in_specs=[SMEM, ANY],
        out_specs=ANY,
        out_shape=jax.ShapeDtypeStruct(shape, bf16),
        scratch_shapes=[pltpu.VMEM(shape, bf16), pltpu.SemaphoreType.DMA((len(spans), slots))],
        compiler_params=pltpu.CompilerParams(vmem_limit_bytes=60 << 20),
        name="route",
    )(deal, x)


def cut_rows(period):
    return [(period // 2, period // 2), (0, period // 2)]


def body(q_new, k_new, v_new, q_bias, k_bias, v_bias, cache_k, cache_v, deal, cache_len):
    slots = lax.axis_size("seq")
    own = lax.axis_index("seq").astype(jnp.int32)
    slot_ids = jnp.arange(slots, dtype=jnp.int32)
    length = jnp.sum(jnp.where(slot_ids == own, cache_len, 0))
    total, q_cols = q_new.shape
    kv_cols = k_new.shape[1]
    kv_heads = kv_cols // HEAD
    packs = q_cols // (2 * kv_cols)
    q_bias, k_bias, v_bias = (x.reshape(1, -1) for x in (q_bias, k_bias, v_bias))
    angles = tables(length, total)
    caches = (cache_k, cache_v)
    meta = jnp.stack([length, own])

    def exchange(x):
        return lax.all_to_all(x, "seq", split_axis=0, concat_axis=0, tiled=True)

    if slots == 8:
        period = total // slots
        chunks = cut_rows(period)
        lead = period // packs
        spread = exchange(deal_pieces(q_new, k_new, v_new, slots, packs))
        deal, meta, angles = lax.optimization_barrier((deal, meta, angles))
        spans = [[(lead + offset, size)] for offset, size in chunks]
        spans[0].insert(0, (0, lead))
        arrived = [exchange(route(deal, spread, span)) for span in spans]
    else:
        inverse = jnp.sum(jnp.where(deal[None, :] == slot_ids[:, None], slot_ids[None, :], 0), axis=1)

        def settle(x):
            spread = exchange(x.reshape(slots, -1, x.shape[1]))
            return exchange(jnp.take(spread, inverse, axis=0))

        period = total // 8
        chunks = cut_rows(period)
        q = settle(q_new).reshape(8, period, q_cols)
        kv = settle(jnp.concatenate([k_new, v_new], axis=1)).reshape(8, packs, period // packs, 2 * kv_cols)
        arrived = [q[:, offset : offset + size] for offset, size in chunks]
        arrived[0] = jnp.concatenate([jnp.concatenate([kv[:, b] for b in range(packs)], axis=2), arrived[0]], axis=1)
    new_k, new_v, norms = fresh_rows(meta, arrived[0], k_bias, v_bias, angles, cache_k, period // packs)
    out = None
    for i, chunk in enumerate(chunks):
        out, stat = attend(
            meta, arrived[i], q_bias, angles, caches, (new_k, new_v), norms, out, *chunk, i == 0, kv_heads
        )
        if i == 0:
            stats = [stat] + [swap_tp(stat, step) for step in range(1, lax.axis_size("tp"))]
    values = jnp.stack(stats)
    place = lax.axis_index("tp") ^ jnp.arange(len(stats), dtype=jnp.int32)
    shares = jnp.sum(values[:, 7, :], axis=1)
    shares = [jnp.sum(jnp.where(place == i, shares, 0.0)) for i in range(len(stats))]
    squares, top = functools.reduce(jnp.add, shares), jnp.max(values[:, 15, :])
    features = q_cols * lax.axis_size("tp")
    norm = jnp.sqrt(squares / features + norm_epsilon)
    return out.reshape(total, q_cols), new_k, new_v, norm.reshape(1), top.reshape(1)


def solution(mesh):
    return jax.shard_map(
        body,
        mesh=mesh,
        in_specs=(
            P("seq", "tp"),
            P("seq", "tp"),
            P("seq", "tp"),
            P("tp"),
            P("tp"),
            P("tp"),
            P("seq", "tp"),
            P("seq", "tp"),
            P(),
            P(),
        ),
        out_specs=(P("seq", "tp"), P("seq", "tp"), P("seq", "tp"), P("seq"), P("seq")),
        check_vma=False,
    )
```

```python
import functools
import math

import jax
import jax.numpy as jnp
from jax import lax
from jax.experimental import pallas as pl
from jax.experimental.pallas import tpu as pltpu
from jax.sharding import PartitionSpec as P

HEAD = 128
LOG2E = 1.4426950408889634
theta_base = 1000000.0
masked_score = -1e30
norm_epsilon = 1e-06
f32, bf16 = jnp.float32, jnp.bfloat16

SAFE = 60.0
ROWS_T = (((1,), (1,)), ((), ()))
PLAIN = (((1,), (0,)), ((), ()))
ANY = pl.BlockSpec(memory_space=pl.ANY)
SMEM = pl.BlockSpec(memory_space=pltpu.SMEM)


def fold(x):
    part = x[:, :HEAD]
    for j in range(1, x.shape[1] // HEAD):
        part = part + x[:, j * HEAD : (j + 1) * HEAD]
    return part


def twice(x):
    return jnp.concatenate([x, x], axis=1)


def attend_kernel(*refs, skip, first, group, wide_block, block, fresh_block, tail):
    meta, arrived, q_bias, cos, sin, ck, cv, nk, nv, norms = refs[:10]
    o_ref, stat, qs, m_s, l_s, acc = refs[-6:]
    length = meta[0]
    scale = HEAD**-0.5 * LOG2E
    pieces, size = arrived.shape[0], arrived.shape[1] - skip
    rows = pieces * size
    for e in range(pieces):
        here = slice(e * size, (e + 1) * size)
        c, s = cos[here, :], sin[here, :]
        for h in range(group):
            column = slice(h * HEAD, (h + 1) * HEAD)
            x = arrived[e, skip : skip + size, column].astype(f32) + q_bias[:, column].astype(f32)
            y = (x * c + pltpu.roll(x, HEAD // 2, 1) * s).astype(bf16).astype(f32)
            z = y * scale
            high = z.astype(bf16)
            at = slice(h * rows + e * size, h * rows + (e + 1) * size)
            qs[at, :HEAD] = high
            qs[at, HEAD:] = (z - high.astype(f32)).astype(bf16)
    high = qs[:, :HEAD].astype(f32)
    lengths = lax.dot_general(
        (high * high).astype(bf16), jnp.ones((HEAD, HEAD), bf16), PLAIN, preferred_element_type=f32
    )
    biggest = jnp.max(lengths.reshape(group * rows // 8, 8, HEAD), axis=0)
    bound = jnp.max(biggest) * jnp.max(norms[...])
    l_s[...] = jnp.zeros(l_s.shape, f32)
    acc[...] = jnp.zeros(acc.shape, f32)
    whole = length // wide_block
    rest = whole * (wide_block // block)
    cached = (length + block - 1) // block

    def causal(heads, width):
        row = lax.broadcasted_iota(jnp.int32, (heads, rows, width), 1).reshape(heads * rows, width)
        return lax.broadcasted_iota(jnp.int32, (heads * rows, width), 1) - row <= first

    @pl.when(bound <= SAFE * SAFE)
    def _():
        def add(k, v, valid):
            weight = jnp.exp2(lax.dot_general(qs[...], twice(k), ROWS_T, preferred_element_type=f32))
            if valid is not None:
                weight = jnp.where(valid, weight, 0.0)
            l_s[...] += fold(weight)
            acc[...] += lax.dot_general(weight.astype(bf16), v, PLAIN, preferred_element_type=f32)

        def full(i, carry):
            at = pl.ds(pl.multiple_of(i * wide_block, wide_block), wide_block)
            add(ck[at, :], cv[at, :], None)
            return carry

        def partial(i, carry):
            at = pl.ds(pl.multiple_of(i * block, block), block)
            key = lax.broadcasted_iota(jnp.int32, (group * rows, block), 1)
            add(ck[at, :], cv[at, :], key < length - i * block)
            return carry

        lax.fori_loop(0, whole, full, 0)
        lax.fori_loop(rest, cached, partial, 0)
        add(nk[...], nv[...], causal(group, fresh_block))

    @pl.when(bound > SAFE * SAFE)
    def _():
        m_s[...] = jnp.full(m_s.shape, masked_score, f32)

        def online(k, v, valid):
            def piece(h, carry):
                at = pl.ds(pl.multiple_of(h * rows, 16), rows)
                scores = lax.dot_general(qs[at, :], twice(k), ROWS_T, preferred_element_type=f32)
                scores = jnp.where(valid, scores, masked_score)
                old = m_s[at, :]
                new = jnp.maximum(old, jnp.max(scores, axis=1, keepdims=True))
                m_s[at, :] = new
                weight = jnp.exp2(scores - jnp.tile(new, (1, k.shape[0] // HEAD)))
                factor = jnp.exp2(old - new)
                l_s[at, :] = l_s[at, :] * factor + fold(weight)
                acc[at, :] = acc[at, :] * factor + lax.dot_general(
                    weight.astype(bf16), v, PLAIN, preferred_element_type=f32
                )
                return carry

            lax.fori_loop(0, group, piece, 0)

        def step(i, carry):
            at = pl.ds(pl.multiple_of(i * block, block), block)
            key = lax.broadcasted_iota(jnp.int32, (rows, block), 1)
            online(ck[at, :], cv[at, :], key < length - i * block)
            return carry

        lax.fori_loop(0, cached, step, 0)
        online(nk[...], nv[...], causal(1, fresh_block))

    squares = jnp.zeros((8, HEAD), f32)
    for h in range(group):
        at = slice(h * rows, (h + 1) * rows)
        mixture = acc[at, :] / jnp.sum(l_s[at, :], axis=1, keepdims=True)
        o_ref[:, h * HEAD : (h + 1) * HEAD] = mixture.astype(bf16)
        end = mixture[rows - 8 :, :]
        squares = squares + end * end
    if tail:
        last = jnp.concatenate([qs[(h + 1) * rows - 16 : (h + 1) * rows, :] for h in range(group)], axis=0)
        old_scores = lax.dot_general(twice(ck[...]), last, ROWS_T, preferred_element_type=f32)
        key = lax.broadcasted_iota(jnp.int32, old_scores.shape, 0)
        old_scores = jnp.where(key < length, old_scores, masked_score)
        new_scores = lax.dot_general(twice(nk[...]), last, ROWS_T, preferred_element_type=f32)
        top = jnp.maximum(
            jnp.max(old_scores.reshape(-1, 8, group * 16), axis=0),
            jnp.max(new_scores.reshape(-1, 8, group * 16), axis=0),
        )
        lane = lax.broadcasted_iota(jnp.int32, top.shape, 1)
        top = jnp.where(lane % 16 == 15, top, masked_score)
        stat[0:8, :] = squares
        stat[8:16, :] = jnp.max(top, axis=(0, 1), keepdims=True) * (1.0 / LOG2E) + jnp.zeros((8, HEAD), f32)
    else:
        stat[...] = jnp.zeros_like(stat)


def attend(meta, arrived, bias, angles, caches, news, norms, out, first, rows, tail, kv_heads):
    pieces, height, q_cols = arrived.shape
    size = rows // pieces
    group = q_cols // HEAD // kv_heads
    wide = group * HEAD
    fresh, cache_rows = news[0].shape[0], caches[0].shape[0]
    fresh_block = min(fresh, -(-(first + rows) // 256) * 256)
    wide_block, block = math.gcd(1024, cache_rows), math.gcd(512, cache_rows)
    column = lambda n, width: pl.BlockSpec((n, width), lambda g, m: (0, g))
    table = pl.BlockSpec((rows, HEAD), lambda g, m: (first // rows, 0))
    given = [] if out is None else [out]
    spec = pltpu.PrefetchScalarGridSpec(
        num_scalar_prefetch=1,
        grid=(kv_heads,),
        in_specs=[
            pl.BlockSpec((pieces, height, wide), lambda g, m: (0, 0, g)), column(1, wide), table, table,
            column(cache_rows, HEAD), column(cache_rows, HEAD),
            column(fresh_block, HEAD), column(fresh_block, HEAD), column(8, HEAD),
        ] + [ANY] * len(given),
        out_specs=[pl.BlockSpec((rows, wide), lambda g, m: (first // rows, g)), column(16, HEAD)],
        scratch_shapes=[
            pltpu.VMEM((group * rows, 2 * HEAD), bf16),
            pltpu.VMEM((group * rows, HEAD), f32),
            pltpu.VMEM((group * rows, HEAD), f32),
            pltpu.VMEM((group * rows, HEAD), f32),
        ],
    )
    work = kv_heads * group * rows * (cache_rows // 2 + fresh)
    return pl.pallas_call(
        functools.partial(
            attend_kernel, skip=height - size, first=first, group=group,
            wide_block=wide_block, block=block, fresh_block=fresh_block, tail=tail,
        ),
        grid_spec=spec,
        out_shape=[
            jax.ShapeDtypeStruct((fresh, q_cols), bf16),
            jax.ShapeDtypeStruct((16, kv_heads * HEAD), f32),
        ],
        input_output_aliases={10: 0} if given else {},
        compiler_params=pltpu.CompilerParams(vmem_limit_bytes=60 << 20),
        cost_estimate=pl.CostEstimate(
            flops=4 * work * HEAD, bytes_accessed=4 * cache_rows * HEAD * kv_heads, transcendentals=work
        ),
        name="attend",
    )(meta, arrived, bias, *angles, *caches, *news, norms, *given)


def tables(length, rows):
    half = HEAD // 2
    frequency = theta_base ** (-2.0 * jnp.arange(half, dtype=f32) / HEAD)
    positions = length + jnp.arange(rows, dtype=jnp.int32)
    angles = positions.astype(f32)[:, None] * frequency[None, :]
    cosine, sine = jnp.cos(angles), jnp.sin(angles)
    return jnp.concatenate([cosine, cosine], 1), jnp.concatenate([-sine, sine], 1)


def longest(keys, valid):
    wide = keys.astype(f32)
    squares = (wide * wide).astype(bf16)
    sums = lax.dot_general(squares, jnp.ones((HEAD, HEAD), bf16), PLAIN, preferred_element_type=f32)
    if valid is not None:
        sums = jnp.where(lax.broadcasted_iota(jnp.int32, sums.shape, 0) < valid, sums, 0.0)
    return jnp.max(sums.reshape(sums.shape[0] // 8, 8, HEAD), axis=0) * 1.05


def fresh_kernel(meta, arrived, k_bias, v_bias, cos, sin, ck, k_out, v_out, norms, *, size, packs):
    length = meta[0]
    cols = k_out.shape[1]
    for e in range(arrived.shape[0]):
        for b in range(packs):
            here = slice((e * packs + b) * size, (e * packs + b + 1) * size)
            raw = arrived[e, :size, 2 * cols * b : 2 * cols * (b + 1)].astype(f32)
            c, s = cos[here, :], sin[here, :]
            for h in range(cols // HEAD):
                column = slice(h * HEAD, (h + 1) * HEAD)
                x = raw[:, column] + k_bias[:, column].astype(f32)
                k_out[here, column] = (x * c + pltpu.roll(x, HEAD // 2, 1) * s).astype(bf16)
            v_out[here, :] = (raw[:, cols:] + v_bias[...].astype(f32)).astype(bf16)
    for h in range(cols // HEAD):
        column = slice(h * HEAD, (h + 1) * HEAD)
        norms[:, column] = jnp.maximum(longest(k_out[:, column], None), longest(ck[:, column], length))


def fresh_rows(meta, arrived, k_bias, v_bias, angles, cache_k, size):
    pieces, _, width = arrived.shape
    cols = k_bias.shape[1]
    packs = width // (2 * cols)
    total = pieces * packs * size
    whole = pl.BlockSpec(memory_space=pltpu.VMEM)
    return pl.pallas_call(
        functools.partial(fresh_kernel, size=size, packs=packs),
        in_specs=[SMEM] + [whole] * 6,
        out_specs=[whole] * 3,
        out_shape=[
            jax.ShapeDtypeStruct((total, cols), bf16),
            jax.ShapeDtypeStruct((total, cols), bf16),
            jax.ShapeDtypeStruct((8, cols), f32),
        ],
        compiler_params=pltpu.CompilerParams(vmem_limit_bytes=32 << 20),
        name="fresh",
    )(meta, arrived, k_bias, v_bias, *angles, cache_k)


def swap_tp(pair, step):
    size = lax.axis_size("tp")
    return lax.ppermute(pair, "tp", [(i, i ^ step) for i in range(size)])


def pass_on(into, back):
    for group in into:
        for copy in group:
            copy.start()
    for group, after in zip(into, back):
        for copy in group:
            copy.wait()
        for copy in after:
            copy.start()
    for after in back:
        for copy in after:
            copy.wait()


def deal_kernel(q, k, v, out, held, sems, out_sems, *, chunks, packs):
    pieces, height, _ = held.shape
    kv_size = height - sum(rows for _, rows in chunks) // pieces
    into = []
    for e in range(pieces):
        copies, base = [], kv_size
        for first, rows in chunks:
            size = rows // pieces
            copies.append((q.at[pl.ds(first + e * size, size)], held.at[e, pl.ds(base, size)]))
            base += size
        for b in range(packs):
            rows = pl.ds((e * packs + b) * kv_size, kv_size)
            for n, x in enumerate((k, v)):
                width = x.shape[1]
                copies.append((x.at[rows], held.at[e, pl.ds(0, kv_size), pl.ds((2 * b + n) * width, width)]))
        into.append([pltpu.make_async_copy(a, b, sems.at[e * len(copies) + n]) for n, (a, b) in enumerate(copies)])
    pass_on(into, [[pltpu.make_async_copy(held.at[e], out.at[e], out_sems.at[e])] for e in range(pieces)])


def deal_pieces(q, k, v, pieces, packs, chunks):
    total, q_cols = q.shape
    shape = (pieces, total // pieces // packs + sum(rows for _, rows in chunks) // pieces, q_cols)
    return pl.pallas_call(
        functools.partial(deal_kernel, chunks=chunks, packs=packs),
        in_specs=[ANY] * 3,
        out_specs=ANY,
        out_shape=jax.ShapeDtypeStruct(shape, bf16),
        scratch_shapes=[
            pltpu.VMEM(shape, bf16),
            pltpu.SemaphoreType.DMA((pieces * (len(chunks) + 2 * packs),)),
            pltpu.SemaphoreType.DMA((pieces,)),
        ],
        compiler_params=pltpu.CompilerParams(vmem_limit_bytes=60 << 20),
        name="deal",
    )(q, k, v)


def route_kernel(deal, x, out, held, sems, out_sems, *, span):
    slots = x.shape[0]
    pass_on(
        [[pltpu.make_async_copy(x.at[s, pl.ds(*span)], held.at[s], sems.at[s])] for s in range(slots)],
        [[pltpu.make_async_copy(held.at[s], out.at[deal[s]], out_sems.at[s])] for s in range(slots)],
    )


def route(deal, x, span):
    slots, _, q_cols = x.shape
    shape = (slots, span[1], q_cols)
    return pl.pallas_call(
        functools.partial(route_kernel, span=span),
        in_specs=[SMEM, ANY],
        out_specs=ANY,
        out_shape=jax.ShapeDtypeStruct(shape, bf16),
        scratch_shapes=[
            pltpu.VMEM(shape, bf16),
            pltpu.SemaphoreType.DMA((slots,)),
            pltpu.SemaphoreType.DMA((slots,)),
        ],
        compiler_params=pltpu.CompilerParams(vmem_limit_bytes=60 << 20),
        name="route",
    )(deal, x)


def cut_rows(total):
    return [(total // 2, total // 2), (0, total // 2)]


def body(q_new, k_new, v_new, q_bias, k_bias, v_bias, cache_k, cache_v, deal, cache_len):
    slots = lax.axis_size("seq")
    own = lax.axis_index("seq").astype(jnp.int32)
    slot_ids = jnp.arange(slots, dtype=jnp.int32)
    length = jnp.sum(jnp.where(slot_ids == own, cache_len, 0))
    total, q_cols = q_new.shape
    kv_cols = k_new.shape[1]
    kv_heads = kv_cols // HEAD
    packs = q_cols // (2 * kv_cols)
    q_bias, k_bias, v_bias = (x.reshape(1, -1) for x in (q_bias, k_bias, v_bias))
    angles = tables(length, total)
    caches = (cache_k, cache_v)
    meta = jnp.stack([length, own])

    def exchange(x):
        return lax.all_to_all(x, "seq", split_axis=0, concat_axis=0, tiled=True)

    pieces = 8
    lead = total // pieces // packs
    chunks = cut_rows(total)
    if slots == pieces:
        spread = exchange(deal_pieces(q_new, k_new, v_new, pieces, packs, chunks))
        deal, meta, angles, q_bias, k_bias, v_bias = lax.optimization_barrier(
            (deal, meta, angles, q_bias, k_bias, v_bias)
        )
        heights = [rows // pieces for _, rows in chunks]
        heights[0] += lead
        spans = [(sum(heights[:i]), heights[i]) for i in range(len(heights))]
        arrived = [exchange(route(deal, spread, span)) for span in spans]
    else:
        inverse = jnp.sum(jnp.where(deal[None, :] == slot_ids[:, None], slot_ids[None, :], 0), axis=1)

        def settle(x):
            spread = exchange(x.reshape(slots, -1, x.shape[1]))
            return exchange(jnp.take(spread, inverse, axis=0))

        q = settle(q_new).reshape(total, q_cols)
        kv = settle(jnp.concatenate([k_new, v_new], axis=1)).reshape(pieces, packs, lead, 2 * kv_cols)
        arrived = [q[first : first + rows].reshape(pieces, -1, q_cols) for first, rows in chunks]
        arrived[0] = jnp.concatenate([jnp.concatenate([kv[:, b] for b in range(packs)], axis=2), arrived[0]], axis=1)
    new_k, new_v, norms = fresh_rows(meta, arrived[0], k_bias, v_bias, angles, cache_k, lead)
    out = None
    for i, chunk in enumerate(chunks):
        out, stat = attend(
            meta, arrived[i], q_bias, angles, caches, (new_k, new_v), norms, out, *chunk, i == 0, kv_heads
        )
        if i == 0:
            stats = [stat] + [swap_tp(stat, step) for step in range(1, lax.axis_size("tp"))]
    values = jnp.stack(stats)
    place = lax.axis_index("tp") ^ jnp.arange(len(stats), dtype=jnp.int32)
    shares = jnp.sum(values[:, 7, :], axis=1)
    shares = [jnp.sum(jnp.where(place == i, shares, 0.0)) for i in range(len(stats))]
    squares, top = functools.reduce(jnp.add, shares), jnp.max(values[:, 15, :])
    features = q_cols * lax.axis_size("tp")
    norm = jnp.sqrt(squares / features + norm_epsilon)
    return out.reshape(total, q_cols), new_k, new_v, norm.reshape(1), top.reshape(1)


def solution(mesh):
    return jax.shard_map(
        body,
        mesh=mesh,
        in_specs=(
            P("seq", "tp"),
            P("seq", "tp"),
            P("seq", "tp"),
            P("tp"),
            P("tp"),
            P("tp"),
            P("seq", "tp"),
            P("seq", "tp"),
            P(),
            P(),
        ),
        out_specs=(P("seq", "tp"), P("seq", "tp"), P("seq", "tp"), P("seq"), P("seq")),
        check_vma=False,
    )
```

```python
import functools
import math

import jax
import jax.numpy as jnp
from jax import lax
from jax.experimental import pallas as pl
from jax.experimental.pallas import tpu as pltpu
from jax.sharding import PartitionSpec as P

HEAD = 128
LOG2E = 1.4426950408889634
theta_base = 1000000.0
masked_score = -1e30
norm_epsilon = 1e-06
f32, bf16 = jnp.float32, jnp.bfloat16

SAFE = 60.0
ROWS_T = (((1,), (1,)), ((), ()))
PLAIN = (((1,), (0,)), ((), ()))
ANY = pl.BlockSpec(memory_space=pl.ANY)
SMEM = pl.BlockSpec(memory_space=pltpu.SMEM)


def fold(x):
    part = x[:, :HEAD]
    for j in range(1, x.shape[1] // HEAD):
        part = part + x[:, j * HEAD : (j + 1) * HEAD]
    return part


def twice(x):
    return jnp.concatenate([x, x], axis=1)


def attend_kernel(*refs, skip, first, group, wide_block, block, fresh_block, tail):
    meta, arrived, q_bias, cos, sin, ck, cv, nk, nv, norms = refs[:10]
    o_ref, stat, qs, m_s, l_s, acc = refs[-6:]
    length = meta[0]
    scale = HEAD**-0.5 * LOG2E
    pieces, size = arrived.shape[0], arrived.shape[1] - skip
    rows = pieces * size
    for e in range(pieces):
        here = slice(e * size, (e + 1) * size)
        c, s = cos[here, :], sin[here, :]
        for h in range(group):
            column = slice(h * HEAD, (h + 1) * HEAD)
            x = arrived[e, skip : skip + size, column].astype(f32) + q_bias[:, column].astype(f32)
            y = (x * c + pltpu.roll(x, HEAD // 2, 1) * s).astype(bf16).astype(f32)
            z = y * scale
            high = z.astype(bf16)
            at = slice(h * rows + e * size, h * rows + (e + 1) * size)
            qs[at, :HEAD] = high
            qs[at, HEAD:] = (z - high.astype(f32)).astype(bf16)
    high = qs[:, :HEAD].astype(f32)
    lengths = lax.dot_general(
        (high * high).astype(bf16), jnp.ones((HEAD, HEAD), bf16), PLAIN, preferred_element_type=f32
    )
    biggest = jnp.max(lengths.reshape(group * rows // 8, 8, HEAD), axis=0)
    bound = jnp.max(biggest) * jnp.max(norms[...])
    l_s[...] = jnp.zeros(l_s.shape, f32)
    acc[...] = jnp.zeros(acc.shape, f32)
    whole = length // wide_block
    rest = whole * (wide_block // block)
    cached = (length + block - 1) // block

    def causal(heads, width):
        row = lax.broadcasted_iota(jnp.int32, (heads, rows, width), 1).reshape(heads * rows, width)
        return lax.broadcasted_iota(jnp.int32, (heads * rows, width), 1) - row <= first

    @pl.when(bound <= SAFE * SAFE)
    def _():
        def add(k, v, valid):
            weight = jnp.exp2(lax.dot_general(qs[...], twice(k), ROWS_T, preferred_element_type=f32))
            if valid is not None:
                weight = jnp.where(valid, weight, 0.0)
            l_s[...] += fold(weight)
            acc[...] += lax.dot_general(weight.astype(bf16), v, PLAIN, preferred_element_type=f32)

        def full(i, carry):
            at = pl.ds(pl.multiple_of(i * wide_block, wide_block), wide_block)
            add(ck[at, :], cv[at, :], None)
            return carry

        def partial(i, carry):
            at = pl.ds(pl.multiple_of(i * block, block), block)
            key = lax.broadcasted_iota(jnp.int32, (group * rows, block), 1)
            add(ck[at, :], cv[at, :], key < length - i * block)
            return carry

        lax.fori_loop(0, whole, full, 0)
        lax.fori_loop(rest, cached, partial, 0)
        add(nk[...], nv[...], causal(group, fresh_block))

    @pl.when(bound > SAFE * SAFE)
    def _():
        m_s[...] = jnp.full(m_s.shape, masked_score, f32)

        def online(k, v, valid):
            def piece(h, carry):
                at = pl.ds(pl.multiple_of(h * rows, 16), rows)
                scores = lax.dot_general(qs[at, :], twice(k), ROWS_T, preferred_element_type=f32)
                scores = jnp.where(valid, scores, masked_score)
                old = m_s[at, :]
                new = jnp.maximum(old, jnp.max(scores, axis=1, keepdims=True))
                m_s[at, :] = new
                weight = jnp.exp2(scores - jnp.tile(new, (1, k.shape[0] // HEAD)))
                factor = jnp.exp2(old - new)
                l_s[at, :] = l_s[at, :] * factor + fold(weight)
                acc[at, :] = acc[at, :] * factor + lax.dot_general(
                    weight.astype(bf16), v, PLAIN, preferred_element_type=f32
                )
                return carry

            lax.fori_loop(0, group, piece, 0)

        def step(i, carry):
            at = pl.ds(pl.multiple_of(i * block, block), block)
            key = lax.broadcasted_iota(jnp.int32, (rows, block), 1)
            online(ck[at, :], cv[at, :], key < length - i * block)
            return carry

        lax.fori_loop(0, cached, step, 0)
        online(nk[...], nv[...], causal(1, fresh_block))

    squares = jnp.zeros((8, HEAD), f32)
    for h in range(group):
        at = slice(h * rows, (h + 1) * rows)
        mixture = acc[at, :] / jnp.sum(l_s[at, :], axis=1, keepdims=True)
        o_ref[:, h * HEAD : (h + 1) * HEAD] = mixture.astype(bf16)
        end = mixture[rows - 8 :, :]
        squares = squares + end * end
    if tail:
        last = jnp.concatenate([qs[(h + 1) * rows - 16 : (h + 1) * rows, :] for h in range(group)], axis=0)
        old_scores = lax.dot_general(twice(ck[...]), last, ROWS_T, preferred_element_type=f32)
        key = lax.broadcasted_iota(jnp.int32, old_scores.shape, 0)
        old_scores = jnp.where(key < length, old_scores, masked_score)
        new_scores = lax.dot_general(twice(nk[...]), last, ROWS_T, preferred_element_type=f32)
        top = jnp.maximum(
            jnp.max(old_scores.reshape(-1, 8, group * 16), axis=0),
            jnp.max(new_scores.reshape(-1, 8, group * 16), axis=0),
        )
        lane = lax.broadcasted_iota(jnp.int32, top.shape, 1)
        top = jnp.where(lane % 16 == 15, top, masked_score)
        stat[0:8, :] = squares
        stat[8:16, :] = jnp.max(top, axis=(0, 1), keepdims=True) * (1.0 / LOG2E) + jnp.zeros((8, HEAD), f32)
    else:
        stat[...] = jnp.zeros_like(stat)


def attend(meta, arrived, bias, angles, caches, news, norms, out, first, rows, tail, kv_heads):
    pieces, height, q_cols = arrived.shape
    size = rows // pieces
    group = q_cols // HEAD // kv_heads
    wide = group * HEAD
    fresh, cache_rows = news[0].shape[0], caches[0].shape[0]
    fresh_block = min(fresh, -(-(first + rows) // 256) * 256)
    wide_block, block = math.gcd(2048, cache_rows), math.gcd(512, cache_rows)
    column = lambda n, width: pl.BlockSpec((n, width), lambda g, m: (0, g))
    table = pl.BlockSpec((rows, HEAD), lambda g, m: (first // rows, 0))
    given = [] if out is None else [out]
    spec = pltpu.PrefetchScalarGridSpec(
        num_scalar_prefetch=1,
        grid=(kv_heads,),
        in_specs=[
            pl.BlockSpec((pieces, height, wide), lambda g, m: (0, 0, g)), column(1, wide), table, table,
            column(cache_rows, HEAD), column(cache_rows, HEAD),
            column(fresh_block, HEAD), column(fresh_block, HEAD), column(8, HEAD),
        ] + [ANY] * len(given),
        out_specs=[pl.BlockSpec((rows, wide), lambda g, m: (first // rows, g)), column(16, HEAD)],
        scratch_shapes=[
            pltpu.VMEM((group * rows, 2 * HEAD), bf16),
            pltpu.VMEM((group * rows, HEAD), f32),
            pltpu.VMEM((group * rows, HEAD), f32),
            pltpu.VMEM((group * rows, HEAD), f32),
        ],
    )
    work = kv_heads * group * rows * (cache_rows // 2 + fresh)
    return pl.pallas_call(
        functools.partial(
            attend_kernel, skip=height - size, first=first, group=group,
            wide_block=wide_block, block=block, fresh_block=fresh_block, tail=tail,
        ),
        grid_spec=spec,
        out_shape=[
            jax.ShapeDtypeStruct((fresh, q_cols), bf16),
            jax.ShapeDtypeStruct((16, kv_heads * HEAD), f32),
        ],
        input_output_aliases={10: 0} if given else {},
        compiler_params=pltpu.CompilerParams(vmem_limit_bytes=60 << 20),
        cost_estimate=pl.CostEstimate(
            flops=4 * work * HEAD, bytes_accessed=4 * cache_rows * HEAD * kv_heads, transcendentals=work
        ),
        name="attend",
    )(meta, arrived, bias, *angles, *caches, *news, norms, *given)


def tables(length, rows):
    half = HEAD // 2
    frequency = theta_base ** (-2.0 * jnp.arange(half, dtype=f32) / HEAD)
    positions = length + jnp.arange(rows, dtype=jnp.int32)
    angles = positions.astype(f32)[:, None] * frequency[None, :]
    cosine, sine = jnp.cos(angles), jnp.sin(angles)
    return jnp.concatenate([cosine, cosine], 1), jnp.concatenate([-sine, sine], 1)


def longest(keys, valid):
    wide = keys.astype(f32)
    squares = (wide * wide).astype(bf16)
    sums = lax.dot_general(squares, jnp.ones((HEAD, HEAD), bf16), PLAIN, preferred_element_type=f32)
    if valid is not None:
        sums = jnp.where(lax.broadcasted_iota(jnp.int32, sums.shape, 0) < valid, sums, 0.0)
    return jnp.max(sums.reshape(sums.shape[0] // 8, 8, HEAD), axis=0) * 1.05


def fresh_kernel(meta, arrived, k_bias, v_bias, cos, sin, ck, k_out, v_out, norms, *, size, packs):
    length = meta[0]
    cols = k_out.shape[1]
    for e in range(arrived.shape[0]):
        for b in range(packs):
            here = slice((e * packs + b) * size, (e * packs + b + 1) * size)
            raw = arrived[e, :size, 2 * cols * b : 2 * cols * (b + 1)].astype(f32)
            c, s = cos[here, :], sin[here, :]
            for h in range(cols // HEAD):
                column = slice(h * HEAD, (h + 1) * HEAD)
                x = raw[:, column] + k_bias[:, column].astype(f32)
                k_out[here, column] = (x * c + pltpu.roll(x, HEAD // 2, 1) * s).astype(bf16)
            v_out[here, :] = (raw[:, cols:] + v_bias[...].astype(f32)).astype(bf16)
    for h in range(cols // HEAD):
        column = slice(h * HEAD, (h + 1) * HEAD)
        norms[:, column] = jnp.maximum(longest(k_out[:, column], None), longest(ck[:, column], length))


def fresh_rows(meta, arrived, k_bias, v_bias, angles, cache_k, size):
    pieces, _, width = arrived.shape
    cols = k_bias.shape[1]
    packs = width // (2 * cols)
    total = pieces * packs * size
    whole = pl.BlockSpec(memory_space=pltpu.VMEM)
    return pl.pallas_call(
        functools.partial(fresh_kernel, size=size, packs=packs),
        in_specs=[SMEM] + [whole] * 6,
        out_specs=[whole] * 3,
        out_shape=[
            jax.ShapeDtypeStruct((total, cols), bf16),
            jax.ShapeDtypeStruct((total, cols), bf16),
            jax.ShapeDtypeStruct((8, cols), f32),
        ],
        compiler_params=pltpu.CompilerParams(vmem_limit_bytes=32 << 20),
        name="fresh",
    )(meta, arrived, k_bias, v_bias, *angles, cache_k)


def swap_tp(pair, step):
    size = lax.axis_size("tp")
    return lax.ppermute(pair, "tp", [(i, i ^ step) for i in range(size)])


def pass_on(into, back):
    for group in into:
        for copy in group:
            copy.start()
    for group, after in zip(into, back):
        for copy in group:
            copy.wait()
        for copy in after:
            copy.start()
    for after in back:
        for copy in after:
            copy.wait()


def deal_kernel(q, k, v, out, held, sems, out_sems, *, chunks, packs):
    pieces, height, _ = held.shape
    kv_size = height - sum(rows for _, rows in chunks) // pieces
    into = []
    for e in range(pieces):
        copies, base = [], kv_size
        for first, rows in chunks:
            size = rows // pieces
            copies.append((q.at[pl.ds(first + e * size, size)], held.at[e, pl.ds(base, size)]))
            base += size
        for b in range(packs):
            rows = pl.ds((e * packs + b) * kv_size, kv_size)
            for n, x in enumerate((k, v)):
                width = x.shape[1]
                copies.append((x.at[rows], held.at[e, pl.ds(0, kv_size), pl.ds((2 * b + n) * width, width)]))
        into.append([pltpu.make_async_copy(a, b, sems.at[e * len(copies) + n]) for n, (a, b) in enumerate(copies)])
    pass_on(into, [[pltpu.make_async_copy(held.at[e], out.at[e], out_sems.at[e])] for e in range(pieces)])


def deal_pieces(q, k, v, pieces, packs, chunks):
    total, q_cols = q.shape
    shape = (pieces, total // pieces // packs + sum(rows for _, rows in chunks) // pieces, q_cols)
    return pl.pallas_call(
        functools.partial(deal_kernel, chunks=chunks, packs=packs),
        in_specs=[ANY] * 3,
        out_specs=ANY,
        out_shape=jax.ShapeDtypeStruct(shape, bf16),
        scratch_shapes=[
            pltpu.VMEM(shape, bf16),
            pltpu.SemaphoreType.DMA((pieces * (len(chunks) + 2 * packs),)),
            pltpu.SemaphoreType.DMA((pieces,)),
        ],
        compiler_params=pltpu.CompilerParams(vmem_limit_bytes=60 << 20),
        name="deal",
    )(q, k, v)


def route_kernel(deal, x, out, held, sems, out_sems, *, span):
    slots = x.shape[0]
    pass_on(
        [[pltpu.make_async_copy(x.at[s, pl.ds(*span)], held.at[s], sems.at[s])] for s in range(slots)],
        [[pltpu.make_async_copy(held.at[s], out.at[deal[s]], out_sems.at[s])] for s in range(slots)],
    )


def route(deal, x, span):
    slots, _, q_cols = x.shape
    shape = (slots, span[1], q_cols)
    return pl.pallas_call(
        functools.partial(route_kernel, span=span),
        in_specs=[SMEM, ANY],
        out_specs=ANY,
        out_shape=jax.ShapeDtypeStruct(shape, bf16),
        scratch_shapes=[
            pltpu.VMEM(shape, bf16),
            pltpu.SemaphoreType.DMA((slots,)),
            pltpu.SemaphoreType.DMA((slots,)),
        ],
        compiler_params=pltpu.CompilerParams(vmem_limit_bytes=60 << 20),
        name="route",
    )(deal, x)


def cut_rows(total):
    return [(total // 2, total // 2), (0, total // 2)]


def finish(stat, q_cols):
    stats = [stat] + [swap_tp(stat, step) for step in range(1, lax.axis_size("tp"))]
    values = jnp.stack(stats)
    place = lax.axis_index("tp") ^ jnp.arange(len(stats), dtype=jnp.int32)
    shares = jnp.sum(values[:, 7, :], axis=1)
    shares = [jnp.sum(jnp.where(place == i, shares, 0.0)) for i in range(len(stats))]
    squares, top = functools.reduce(jnp.add, shares), jnp.max(values[:, 15, :])
    features = q_cols * lax.axis_size("tp")
    norm = jnp.sqrt(squares / features + norm_epsilon)
    return norm, top


def body(q_new, k_new, v_new, q_bias, k_bias, v_bias, cache_k, cache_v, deal, cache_len):
    slots = lax.axis_size("seq")
    own = lax.axis_index("seq").astype(jnp.int32)
    slot_ids = jnp.arange(slots, dtype=jnp.int32)
    length = jnp.sum(jnp.where(slot_ids == own, cache_len, 0))
    total, q_cols = q_new.shape
    kv_cols = k_new.shape[1]
    kv_heads = kv_cols // HEAD
    packs = q_cols // (2 * kv_cols)
    q_bias, k_bias, v_bias = (x.reshape(1, -1) for x in (q_bias, k_bias, v_bias))
    angles = tables(length, total)
    caches = (cache_k, cache_v)
    meta = jnp.stack([length, own])

    def exchange(x):
        return lax.all_to_all(x, "seq", split_axis=0, concat_axis=0, tiled=True)

    pieces = 8
    lead = total // pieces // packs
    chunks = cut_rows(total)
    if slots == pieces:
        spread = exchange(deal_pieces(q_new, k_new, v_new, pieces, packs, chunks))
        deal, meta, angles, q_bias, k_bias, v_bias = lax.optimization_barrier(
            (deal, meta, angles, q_bias, k_bias, v_bias)
        )
        heights = [rows // pieces for _, rows in chunks]
        heights[0] += lead
        spans = [(sum(heights[:i]), heights[i]) for i in range(len(heights))]
        arrived = [exchange(route(deal, spread, span)) for span in spans]
    else:
        inverse = jnp.sum(jnp.where(deal[None, :] == slot_ids[:, None], slot_ids[None, :], 0), axis=1)

        def settle(x):
            spread = exchange(x.reshape(slots, -1, x.shape[1]))
            return exchange(jnp.take(spread, inverse, axis=0))

        q = settle(q_new).reshape(total, q_cols)
        kv = settle(jnp.concatenate([k_new, v_new], axis=1)).reshape(pieces, packs, lead, 2 * kv_cols)
        arrived = [q[first : first + rows].reshape(pieces, -1, q_cols) for first, rows in chunks]
        arrived[0] = jnp.concatenate([jnp.concatenate([kv[:, b] for b in range(packs)], axis=2), arrived[0]], axis=1)
    new_k, new_v, norms = fresh_rows(meta, arrived[0], k_bias, v_bias, angles, cache_k, lead)
    out = None
    for i, chunk in enumerate(chunks):
        out, stat = attend(
            meta, arrived[i], q_bias, angles, caches, (new_k, new_v), norms, out, *chunk, i == 0, kv_heads
        )
        if i == 0:
            norm, top = finish(stat, q_cols)
            meta, norm, top = lax.optimization_barrier((meta, norm, top))
    return out.reshape(total, q_cols), new_k, new_v, norm.reshape(1), top.reshape(1)


def solution(mesh):
    return jax.shard_map(
        body,
        mesh=mesh,
        in_specs=(
            P("seq", "tp"),
            P("seq", "tp"),
            P("seq", "tp"),
            P("tp"),
            P("tp"),
            P("tp"),
            P("seq", "tp"),
            P("seq", "tp"),
            P(),
            P(),
        ),
        out_specs=(P("seq", "tp"), P("seq", "tp"), P("seq", "tp"), P("seq"), P("seq")),
        check_vma=False,
    )
```

```python
import functools
import math

import jax
import jax.numpy as jnp
from jax import lax
from jax.experimental import pallas as pl
from jax.experimental.pallas import tpu as pltpu
from jax.sharding import PartitionSpec as P

HEAD = 128
LOG2E = 1.4426950408889634
theta_base = 1000000.0
masked_score = -1e30
norm_epsilon = 1e-06
f32, bf16 = jnp.float32, jnp.bfloat16

SAFE = 60.0
ROWS_T = (((1,), (1,)), ((), ()))
PLAIN = (((1,), (0,)), ((), ()))
ANY = pl.BlockSpec(memory_space=pl.ANY)
SMEM = pl.BlockSpec(memory_space=pltpu.SMEM)


def fold(x):
    part = x[:, :HEAD]
    for j in range(1, x.shape[1] // HEAD):
        part = part + x[:, j * HEAD : (j + 1) * HEAD]
    return part


def twice(x):
    return jnp.concatenate([x, x], axis=1)


def attend_kernel(*refs, skip, first, group, wide_block, block, fresh_block, tail):
    meta, arrived, q_bias, cos, sin, ck, cv, nk, nv, norms = refs[:10]
    o_ref, stat, qs, m_s, l_s, acc = refs[-6:]
    length = meta[0]
    scale = HEAD**-0.5 * LOG2E
    pieces, size = arrived.shape[0], arrived.shape[1] - skip
    rows = pieces * size
    for e in range(pieces):
        here = slice(e * size, (e + 1) * size)
        c, s = cos[here, :], sin[here, :]
        for h in range(group):
            column = slice(h * HEAD, (h + 1) * HEAD)
            x = arrived[e, skip : skip + size, column].astype(f32) + q_bias[:, column].astype(f32)
            y = (x * c + pltpu.roll(x, HEAD // 2, 1) * s).astype(bf16).astype(f32)
            z = y * scale
            high = z.astype(bf16)
            at = slice(h * rows + e * size, h * rows + (e + 1) * size)
            qs[at, :HEAD] = high
            qs[at, HEAD:] = (z - high.astype(f32)).astype(bf16)
    high = qs[:, :HEAD].astype(f32)
    lengths = lax.dot_general(
        (high * high).astype(bf16), jnp.ones((HEAD, HEAD), bf16), PLAIN, preferred_element_type=f32
    )
    biggest = jnp.max(lengths.reshape(group * rows // 8, 8, HEAD), axis=0)
    bound = jnp.max(biggest) * jnp.max(norms[...])
    l_s[...] = jnp.zeros(l_s.shape, f32)
    acc[...] = jnp.zeros(acc.shape, f32)
    whole = length // wide_block
    rest = whole * (wide_block // block)
    cached = (length + block - 1) // block

    def causal(heads, width):
        row = lax.broadcasted_iota(jnp.int32, (heads, rows, width), 1).reshape(heads * rows, width)
        return lax.broadcasted_iota(jnp.int32, (heads * rows, width), 1) - row <= first

    @pl.when(bound <= SAFE * SAFE)
    def _():
        def add(k, v, valid):
            weight = jnp.exp2(lax.dot_general(qs[...], twice(k), ROWS_T, preferred_element_type=f32))
            if valid is not None:
                weight = jnp.where(valid, weight, 0.0)
            l_s[...] += fold(weight)
            acc[...] += lax.dot_general(weight.astype(bf16), v, PLAIN, preferred_element_type=f32)

        def full(i, carry):
            at = pl.ds(pl.multiple_of(i * wide_block, wide_block), wide_block)
            add(ck[at, :], cv[at, :], None)
            return carry

        def partial(i, carry):
            at = pl.ds(pl.multiple_of(i * block, block), block)
            key = lax.broadcasted_iota(jnp.int32, (group * rows, block), 1)
            add(ck[at, :], cv[at, :], key < length - i * block)
            return carry

        lax.fori_loop(0, whole, full, 0)
        lax.fori_loop(rest, cached, partial, 0)
        add(nk[...], nv[...], causal(group, fresh_block))

    @pl.when(bound > SAFE * SAFE)
    def _():
        m_s[...] = jnp.full(m_s.shape, masked_score, f32)

        def online(k, v, valid):
            def piece(h, carry):
                at = pl.ds(pl.multiple_of(h * rows, 16), rows)
                scores = lax.dot_general(qs[at, :], twice(k), ROWS_T, preferred_element_type=f32)
                scores = jnp.where(valid, scores, masked_score)
                old = m_s[at, :]
                new = jnp.maximum(old, jnp.max(scores, axis=1, keepdims=True))
                m_s[at, :] = new
                weight = jnp.exp2(scores - jnp.tile(new, (1, k.shape[0] // HEAD)))
                factor = jnp.exp2(old - new)
                l_s[at, :] = l_s[at, :] * factor + fold(weight)
                acc[at, :] = acc[at, :] * factor + lax.dot_general(
                    weight.astype(bf16), v, PLAIN, preferred_element_type=f32
                )
                return carry

            lax.fori_loop(0, group, piece, 0)

        def step(i, carry):
            at = pl.ds(pl.multiple_of(i * block, block), block)
            key = lax.broadcasted_iota(jnp.int32, (rows, block), 1)
            online(ck[at, :], cv[at, :], key < length - i * block)
            return carry

        lax.fori_loop(0, cached, step, 0)
        online(nk[...], nv[...], causal(1, fresh_block))

    squares = jnp.zeros((8, HEAD), f32)
    for h in range(group):
        at = slice(h * rows, (h + 1) * rows)
        mixture = acc[at, :] / jnp.sum(l_s[at, :], axis=1, keepdims=True)
        o_ref[:, h * HEAD : (h + 1) * HEAD] = mixture.astype(bf16)
        end = mixture[rows - 8 :, :]
        squares = squares + end * end
    if tail:
        last = jnp.concatenate([qs[(h + 1) * rows - 16 : (h + 1) * rows, :] for h in range(group)], axis=0)
        old_scores = lax.dot_general(twice(ck[...]), last, ROWS_T, preferred_element_type=f32)
        key = lax.broadcasted_iota(jnp.int32, old_scores.shape, 0)
        old_scores = jnp.where(key < length, old_scores, masked_score)
        new_scores = lax.dot_general(twice(nk[...]), last, ROWS_T, preferred_element_type=f32)
        top = jnp.maximum(
            jnp.max(old_scores.reshape(-1, 8, group * 16), axis=0),
            jnp.max(new_scores.reshape(-1, 8, group * 16), axis=0),
        )
        lane = lax.broadcasted_iota(jnp.int32, top.shape, 1)
        top = jnp.where(lane % 16 == 15, top, masked_score)
        stat[0:8, :] = squares
        stat[8:16, :] = jnp.max(top, axis=(0, 1), keepdims=True) * (1.0 / LOG2E) + jnp.zeros((8, HEAD), f32)
    else:
        stat[...] = jnp.zeros_like(stat)


def attend(meta, arrived, bias, angles, caches, news, norms, out, first, rows, tail, kv_heads):
    pieces, height, q_cols = arrived.shape
    size = rows // pieces
    group = q_cols // HEAD // kv_heads
    wide = group * HEAD
    fresh, cache_rows = news[0].shape[0], caches[0].shape[0]
    fresh_block = min(fresh, -(-(first + rows) // 256) * 256)
    wide_block, block = math.gcd(2048, cache_rows), math.gcd(512, cache_rows)
    column = lambda n, width: pl.BlockSpec((n, width), lambda g, m: (0, g))
    table = pl.BlockSpec((rows, HEAD), lambda g, m: (first // rows, 0))
    given = [] if out is None else [out]
    spec = pltpu.PrefetchScalarGridSpec(
        num_scalar_prefetch=1,
        grid=(kv_heads,),
        in_specs=[
            pl.BlockSpec((pieces, height, wide), lambda g, m: (0, 0, g)), column(1, wide), table, table,
            column(cache_rows, HEAD), column(cache_rows, HEAD),
            column(fresh_block, HEAD), column(fresh_block, HEAD), column(8, HEAD),
        ] + [ANY] * len(given),
        out_specs=[pl.BlockSpec((rows, wide), lambda g, m: (first // rows, g)), column(16, HEAD)],
        scratch_shapes=[
            pltpu.VMEM((group * rows, 2 * HEAD), bf16),
            pltpu.VMEM((group * rows, HEAD), f32),
            pltpu.VMEM((group * rows, HEAD), f32),
            pltpu.VMEM((group * rows, HEAD), f32),
        ],
    )
    work = kv_heads * group * rows * (cache_rows // 2 + fresh)
    return pl.pallas_call(
        functools.partial(
            attend_kernel, skip=height - size, first=first, group=group,
            wide_block=wide_block, block=block, fresh_block=fresh_block, tail=tail,
        ),
        grid_spec=spec,
        out_shape=[
            jax.ShapeDtypeStruct((fresh, q_cols), bf16),
            jax.ShapeDtypeStruct((16, kv_heads * HEAD), f32),
        ],
        input_output_aliases={10: 0} if given else {},
        compiler_params=pltpu.CompilerParams(vmem_limit_bytes=60 << 20),
        cost_estimate=pl.CostEstimate(
            flops=4 * work * HEAD, bytes_accessed=4 * cache_rows * HEAD * kv_heads, transcendentals=work
        ),
        name="attend",
    )(meta, arrived, bias, *angles, *caches, *news, norms, *given)


def tables(length, rows):
    half = HEAD // 2
    frequency = theta_base ** (-2.0 * jnp.arange(half, dtype=f32) / HEAD)
    positions = length + jnp.arange(rows, dtype=jnp.int32)
    angles = positions.astype(f32)[:, None] * frequency[None, :]
    cosine, sine = jnp.cos(angles), jnp.sin(angles)
    return jnp.concatenate([cosine, cosine], 1), jnp.concatenate([-sine, sine], 1)


def longest(keys, valid):
    wide = keys.astype(f32)
    squares = (wide * wide).astype(bf16)
    sums = lax.dot_general(squares, jnp.ones((HEAD, HEAD), bf16), PLAIN, preferred_element_type=f32)
    if valid is not None:
        sums = jnp.where(lax.broadcasted_iota(jnp.int32, sums.shape, 0) < valid, sums, 0.0)
    return jnp.max(sums.reshape(sums.shape[0] // 8, 8, HEAD), axis=0) * 1.05


def fresh_kernel(meta, arrived, k_bias, v_bias, cos, sin, ck, k_out, v_out, norms, *, size, packs):
    length = meta[0]
    cols = k_out.shape[1]
    for e in range(arrived.shape[0]):
        for b in range(packs):
            here = slice((e * packs + b) * size, (e * packs + b + 1) * size)
            raw = arrived[e, :size, 2 * cols * b : 2 * cols * (b + 1)].astype(f32)
            c, s = cos[here, :], sin[here, :]
            for h in range(cols // HEAD):
                column = slice(h * HEAD, (h + 1) * HEAD)
                x = raw[:, column] + k_bias[:, column].astype(f32)
                k_out[here, column] = (x * c + pltpu.roll(x, HEAD // 2, 1) * s).astype(bf16)
            v_out[here, :] = (raw[:, cols:] + v_bias[...].astype(f32)).astype(bf16)
    for h in range(cols // HEAD):
        column = slice(h * HEAD, (h + 1) * HEAD)
        norms[:, column] = jnp.maximum(longest(k_out[:, column], None), longest(ck[:, column], length))


def fresh_rows(meta, arrived, k_bias, v_bias, angles, cache_k, size):
    pieces, _, width = arrived.shape
    cols = k_bias.shape[1]
    packs = width // (2 * cols)
    total = pieces * packs * size
    whole = pl.BlockSpec(memory_space=pltpu.VMEM)
    return pl.pallas_call(
        functools.partial(fresh_kernel, size=size, packs=packs),
        in_specs=[SMEM] + [whole] * 6,
        out_specs=[whole] * 3,
        out_shape=[
            jax.ShapeDtypeStruct((total, cols), bf16),
            jax.ShapeDtypeStruct((total, cols), bf16),
            jax.ShapeDtypeStruct((8, cols), f32),
        ],
        compiler_params=pltpu.CompilerParams(vmem_limit_bytes=32 << 20),
        name="fresh",
    )(meta, arrived, k_bias, v_bias, *angles, cache_k)


def swap_tp(pair, step):
    size = lax.axis_size("tp")
    return lax.ppermute(pair, "tp", [(i, i ^ step) for i in range(size)])


def pass_on(into, back):
    for group in into:
        for copy in group:
            copy.start()
    for group, after in zip(into, back):
        for copy in group:
            copy.wait()
        for copy in after:
            copy.start()
    for after in back:
        for copy in after:
            copy.wait()


def deal_kernel(q, k, v, out, held, sems, out_sems, *, chunks, packs):
    pieces, height, _ = held.shape
    kv_size = height - sum(rows for _, rows in chunks) // pieces
    into = []
    for e in range(pieces):
        copies, base = [], kv_size
        for first, rows in chunks:
            size = rows // pieces
            copies.append((q.at[pl.ds(first + e * size, size)], held.at[e, pl.ds(base, size)]))
            base += size
        for b in range(packs):
            rows = pl.ds((e * packs + b) * kv_size, kv_size)
            for n, x in enumerate((k, v)):
                width = x.shape[1]
                copies.append((x.at[rows], held.at[e, pl.ds(0, kv_size), pl.ds((2 * b + n) * width, width)]))
        into.append([pltpu.make_async_copy(a, b, sems.at[e * len(copies) + n]) for n, (a, b) in enumerate(copies)])
    pass_on(into, [[pltpu.make_async_copy(held.at[e], out.at[e], out_sems.at[e])] for e in range(pieces)])


def deal_pieces(q, k, v, pieces, packs, chunks):
    total, q_cols = q.shape
    shape = (pieces, total // pieces // packs + sum(rows for _, rows in chunks) // pieces, q_cols)
    return pl.pallas_call(
        functools.partial(deal_kernel, chunks=chunks, packs=packs),
        in_specs=[ANY] * 3,
        out_specs=ANY,
        out_shape=jax.ShapeDtypeStruct(shape, bf16),
        scratch_shapes=[
            pltpu.VMEM(shape, bf16),
            pltpu.SemaphoreType.DMA((pieces * (len(chunks) + 2 * packs),)),
            pltpu.SemaphoreType.DMA((pieces,)),
        ],
        compiler_params=pltpu.CompilerParams(vmem_limit_bytes=60 << 20),
        name="deal",
    )(q, k, v)


def route_kernel(deal, x, out, held, sems, out_sems, *, span):
    slots = x.shape[0]
    pass_on(
        [[pltpu.make_async_copy(x.at[s, pl.ds(*span)], held.at[s], sems.at[s])] for s in range(slots)],
        [[pltpu.make_async_copy(held.at[s], out.at[deal[s]], out_sems.at[s])] for s in range(slots)],
    )


def route(deal, x, span):
    slots, _, q_cols = x.shape
    shape = (slots, span[1], q_cols)
    return pl.pallas_call(
        functools.partial(route_kernel, span=span),
        in_specs=[SMEM, ANY],
        out_specs=ANY,
        out_shape=jax.ShapeDtypeStruct(shape, bf16),
        scratch_shapes=[
            pltpu.VMEM(shape, bf16),
            pltpu.SemaphoreType.DMA((slots,)),
            pltpu.SemaphoreType.DMA((slots,)),
        ],
        compiler_params=pltpu.CompilerParams(vmem_limit_bytes=60 << 20),
        name="route",
    )(deal, x)


def cut_rows(total):
    return [(total // 2, total // 2), (0, total // 2)]


def body(q_new, k_new, v_new, q_bias, k_bias, v_bias, cache_k, cache_v, deal, cache_len):
    slots = lax.axis_size("seq")
    own = lax.axis_index("seq").astype(jnp.int32)
    slot_ids = jnp.arange(slots, dtype=jnp.int32)
    length = jnp.sum(jnp.where(slot_ids == own, cache_len, 0))
    total, q_cols = q_new.shape
    kv_cols = k_new.shape[1]
    kv_heads = kv_cols // HEAD
    packs = q_cols // (2 * kv_cols)
    q_bias, k_bias, v_bias = (x.reshape(1, -1) for x in (q_bias, k_bias, v_bias))
    angles = tables(length, total)
    caches = (cache_k, cache_v)
    meta = jnp.stack([length, own])

    def exchange(x):
        return lax.all_to_all(x, "seq", split_axis=0, concat_axis=0, tiled=True)

    pieces = 8
    lead = total // pieces // packs
    chunks = cut_rows(total)
    if slots == pieces:
        spread = exchange(deal_pieces(q_new, k_new, v_new, pieces, packs, chunks))
        deal, meta, angles, q_bias, k_bias, v_bias = lax.optimization_barrier(
            (deal, meta, angles, q_bias, k_bias, v_bias)
        )
        heights = [rows // pieces for _, rows in chunks]
        heights[0] += lead
        spans = [(sum(heights[:i]), heights[i]) for i in range(len(heights))]
        arrived = [exchange(route(deal, spread, span)) for span in spans]
    else:
        inverse = jnp.sum(jnp.where(deal[None, :] == slot_ids[:, None], slot_ids[None, :], 0), axis=1)

        def settle(x):
            spread = exchange(x.reshape(slots, -1, x.shape[1]))
            return exchange(jnp.take(spread, inverse, axis=0))

        q = settle(q_new).reshape(total, q_cols)
        kv = settle(jnp.concatenate([k_new, v_new], axis=1)).reshape(pieces, packs, lead, 2 * kv_cols)
        arrived = [q[first : first + rows].reshape(pieces, -1, q_cols) for first, rows in chunks]
        arrived[0] = jnp.concatenate([jnp.concatenate([kv[:, b] for b in range(packs)], axis=2), arrived[0]], axis=1)
    new_k, new_v, norms = fresh_rows(meta, arrived[0], k_bias, v_bias, angles, cache_k, lead)
    out = None
    for i, chunk in enumerate(chunks):
        out, stat = attend(
            meta, arrived[i], q_bias, angles, caches, (new_k, new_v), norms, out, *chunk, i == 0, kv_heads
        )
        if i == 0:
            stats = [stat] + [swap_tp(stat, step) for step in range(1, lax.axis_size("tp"))]
    values = jnp.stack(stats)
    place = lax.axis_index("tp") ^ jnp.arange(len(stats), dtype=jnp.int32)
    shares = jnp.sum(values[:, 7, :], axis=1)
    shares = [jnp.sum(jnp.where(place == i, shares, 0.0)) for i in range(len(stats))]
    squares, top = functools.reduce(jnp.add, shares), jnp.max(values[:, 15, :])
    features = q_cols * lax.axis_size("tp")
    norm = jnp.sqrt(squares / features + norm_epsilon)
    return out.reshape(total, q_cols), new_k, new_v, norm.reshape(1), top.reshape(1)


def solution(mesh):
    return jax.shard_map(
        body,
        mesh=mesh,
        in_specs=(
            P("seq", "tp"),
            P("seq", "tp"),
            P("seq", "tp"),
            P("tp"),
            P("tp"),
            P("tp"),
            P("seq", "tp"),
            P("seq", "tp"),
            P(),
            P(),
        ),
        out_specs=(P("seq", "tp"), P("seq", "tp"), P("seq", "tp"), P("seq"), P("seq")),
        check_vma=False,
    )
```
